128 devices in a mesh: rep: 2 (over z_lo), exp: 64 (over z_hi, x, y, core).
Axes of the slice: x: 4, y: 4, z: 4 (z_hi: 2, z_lo: 2; z = z_hi * 2 + z_lo), core: 2. Of those that a mesh axis runs over, the one named last changes fastest.
Arguments:
- tokens: bfloat16 [512, 256, 1280], P(('rep', 'exp')), may hold values from -19 to 19
- slot_params: bfloat16 [1280, 64], replicated, may hold values from -1 to 1
- expert_in: bfloat16 [64, 1280, 2560], P('exp'), may hold values from -0.15625 to 0.15625
- expert_out: bfloat16 [64, 2560, 1280], P('exp'), may hold values from -0.125 to 0.125
- grad_out: bfloat16 [512, 256, 1280], P(('rep', 'exp')), may hold values from -6 to 6
Outputs:
- grad_tokens: bfloat16 [512, 256, 1280], P(('rep', 'exp'))
- grad_params: float32 [1280, 64], replicated
- grad_expert_in: bfloat16 [64, 1280, 2560], P('exp', 'rep')
- grad_expert_out: bfloat16 [64, 2560, 1280], P('exp', 'rep')
The draws below stay inside these ranges and needn't reach their ends.
All inputs are finite; a program needn't handle non-finite values.
Results may differ from the reference program's by a relative error of at most 0.0093.
Values may be sent and summed in bfloat16 or wider, within the bound.
A program may use at most 128 MiB of HBM per device.

```python
import math
import jax
import jax.numpy as jnp
from jax import lax

D = 1280
F = 2560
M = 256
SLOTS = 64
IMAGES = 512
N_REP = 2


def draw_slot_params(key, part):
    key = jax.random.fold_in(key, 5)
    second_key = jax.random.fold_in(key, 1)
    values = jax.random.normal(second_key, (D, SLOTS), jnp.float32) / math.sqrt(D)
    return values.astype(jnp.bfloat16)


def draw_tokens(key, part):
    key = jax.random.fold_in(key, 9)
    keys_list = jax.random.split(key, 1)
    values = jnp.clip(jax.random.normal(keys_list[0], (IMAGES, M, D), jnp.float32), -6.0, 6.0)
    return values.astype(jnp.bfloat16)


def level_of(key, dims, cuts, smallest, largest):
    factor_of, own = 1.0, jax.random.fold_in(key, 6)
    for axis_at, blocks in cuts:
        draws = jnp.exp(jax.random.uniform(jax.random.fold_in(own, axis_at), (blocks,), jnp.float32, smallest / len(cuts), largest / len(cuts)))
        factor_of = factor_of * jnp.repeat(draws, dims[axis_at] // blocks).reshape([-1 if axis == axis_at else 1 for axis in range(len(dims))])
    return factor_of


def normal_values(stream_key, dims, spread, most, cuts=(), dtype=jnp.bfloat16):
    result = jax.random.normal(stream_key, dims, jnp.float32) * spread
    if len(cuts) > 0:
        result = level_of(stream_key, dims, cuts, -0.22, 0.18) * result
    return jnp.clip(result, min=-most, max=most).astype(dtype)


def setup_inputs(seed: int = 0) -> dict:
    splits = jax.random.split(jax.random.key(seed), 6)
    return {
        "tokens": draw_tokens(jax.random.fold_in(splits[5], 71), 0),
        "slot_params": draw_slot_params(jax.random.fold_in(splits[5], 71), 0),
        "expert_in": normal_values(splits[2], (SLOTS, D, F), D ** -0.5, 0.15625, ((0, 64),)),
        "expert_out": normal_values(splits[3], (SLOTS, F, D), F ** -0.5, 0.125, ((0, 64),)),
        "grad_out": normal_values(splits[4], (IMAGES, M, D), 1.0, 6.0, ((0, 128),)),
    }


GELU_C = math.sqrt(2.0 / math.pi)
CUBIC = 0.044715

def gelu_tanh(values):
    inner = GELU_C * (values + CUBIC * values * values * values)
    return 0.5 * values * (1.0 + jnp.tanh(inner))

def gelu_slope(values):
    tangent = jnp.tanh(GELU_C * (values + CUBIC * values * values * values))
    return 0.5 * (1.0 + tangent) + 0.5 * values * (1.0 - tangent * tangent) * GELU_C * (1.0 + 3.0 * CUBIC * values * values)

def replica_sum(left, right):
    left_wide = left.astype(jnp.float32).reshape(N_REP, -1, left.shape[1])
    right_wide = right.astype(jnp.float32).reshape(N_REP, -1, right.shape[1])
    terms = jnp.einsum('rka,rkb->rab', left_wide, right_wide).astype(jnp.bfloat16)
    terms = lax.optimization_barrier(terms)
    return lax.optimization_barrier(jnp.sum(terms.astype(jnp.float32), axis=0)).astype(jnp.bfloat16)

def expert_pass(operands):
    rows_in, rows_grad, weight_in, weight_out = operands
    preact = jnp.dot(rows_in, weight_in, preferred_element_type=jnp.float32)
    activations = gelu_tanh(preact).astype(jnp.bfloat16)
    rows_out = jnp.dot(activations, weight_out, preferred_element_type=jnp.float32).astype(jnp.bfloat16)
    d_acts = jnp.dot(rows_grad, weight_out.T, preferred_element_type=jnp.float32)
    d_hidden = (d_acts * gelu_slope(preact)).astype(jnp.bfloat16)
    d_rows = jnp.dot(d_hidden, weight_in.T, preferred_element_type=jnp.float32).astype(jnp.bfloat16)
    return (rows_out, d_rows, replica_sum(rows_in, d_hidden), replica_sum(activations, rows_grad))

def reference(tokens, slot_params, expert_in, expert_out, grad_out):
    tokens_wide = tokens.astype(jnp.float32)
    grads_wide = grad_out.astype(jnp.float32)
    params_wide = slot_params.astype(jnp.float32)
    logits = jnp.einsum('bmd,ds->bsm', tokens_wide, params_wide)
    dispatch = jax.nn.softmax(logits, axis=2)
    combine = jax.nn.softmax(logits, axis=1)
    dispatch_low = dispatch.astype(jnp.bfloat16)
    combine_low = combine.astype(jnp.bfloat16)
    slot_in = jnp.einsum('bsm,bmd->bsd', dispatch_low.astype(jnp.float32), tokens_wide).astype(jnp.bfloat16)
    slot_grad = jnp.einsum('bsm,bmd->bsd', combine_low.astype(jnp.float32), grads_wide).astype(jnp.bfloat16)
    slot_out, d_slot_in, grad_expert_in, grad_expert_out = lax.map(expert_pass, (jnp.swapaxes(slot_in, 0, 1), jnp.swapaxes(slot_grad, 0, 1), expert_in, expert_out))
    slot_out = jnp.swapaxes(slot_out, 0, 1).astype(jnp.float32)
    d_slot_in = jnp.swapaxes(d_slot_in, 0, 1).astype(jnp.float32)
    d_combine = jnp.einsum('bmd,bsd->bsm', grads_wide, slot_out)
    d_dispatch = jnp.einsum('bmd,bsd->bsm', tokens_wide, d_slot_in)
    d_logits = combine * (d_combine - lax.optimization_barrier(jnp.sum(combine * d_combine, axis=1, keepdims=True)))
    d_logits = d_logits + dispatch * (d_dispatch - lax.optimization_barrier(jnp.sum(dispatch * d_dispatch, axis=2, keepdims=True)))
    d_logits_low = d_logits.astype(jnp.bfloat16).astype(jnp.float32)
    grad_tokens = jnp.einsum('bsm,bsd->bmd', dispatch_low.astype(jnp.float32), d_slot_in)
    grad_tokens = grad_tokens + jnp.einsum('bsm,ds->bmd', d_logits_low, params_wide)
    grad_params = jnp.einsum('bmd,bsm->ds', tokens_wide, d_logits_low)
    return (grad_tokens.astype(jnp.bfloat16), grad_params, grad_expert_in, grad_expert_out)
```

```python
import math

import jax
import jax.numpy as jnp
from jax import lax
from jax.experimental import pallas as pl
from jax.experimental.pallas import tpu as pltpu
from jax.sharding import PartitionSpec as P

GELU_C = math.sqrt(2.0 / math.pi)
CUBIC = 0.044715
MESH = pl.DeviceIdType.MESH

D = 1280
F = 2560
M = 256
S = 64
B = 4
R = S * B
HALF = D // 2
BF = jnp.bfloat16
F32 = jnp.float32

NT = (((1,), (1,)), ((), ()))


def dot(a, b):
    return jnp.dot(a, b, preferred_element_type=F32)


def dot_nt(a, b):
    return lax.dot_general(a, b, NT, preferred_element_type=F32)


def pack(first, second):
    width = first.shape[1]
    a = first.reshape(R // 8, 8, width)
    g = second.reshape(R // 8, 8, width)
    low = lax.broadcasted_iota(jnp.int32, a.shape, 1) < 4
    even = jnp.where(low, a, pltpu.roll(g, 4, 1))
    odd = jnp.where(low, pltpu.roll(a, 4, 1), g)
    return even, odd


def unpack(even, odd):
    low = lax.broadcasted_iota(jnp.int32, even.shape, 1) < 4
    a = jnp.where(low, even, pltpu.roll(odd, 4, 1))
    g = jnp.where(low, pltpu.roll(even, 4, 1), odd)
    return a.reshape(R, -1), g.reshape(R, -1)


def by_parity(buf):
    return buf.reshape(S // 2, 2, 16, HALF)


def store_message(msg, p, first, second):
    even, odd = pack(first, second)
    msg = by_parity(msg)
    at = pl.ds(pl.multiple_of(p * 128, 128), 128)
    for j, v in enumerate((even, odd)):
        rows = jnp.concatenate([v[:, :, :128], v[:, :, 128:]], axis=1)
        msg[:, j, :, at] = rows.astype(BF)


def load_message(rcv, p):
    rcv = by_parity(rcv)
    at = pl.ds(pl.multiple_of(p * 128, 128), 128)
    sides = []
    for j in range(2):
        rows = rcv[:, j, :, at].astype(F32)
        sides.append(jnp.concatenate([rows[:, :8], rows[:, 8:]], axis=2))
    return unpack(sides[0], sides[1])


def gelu_both(v):
    u = v * v
    t = jnp.tanh(GELU_C * (v + CUBIC * v * u))
    half = 0.5 * (1.0 + t)
    slope = half + 0.5 * v * (1.0 - t * t) * (GELU_C * (1.0 + 3.0 * CUBIC * u))
    return half * v, slope


def kernel(
    tok_hbm, sp_hbm, win_hbm, wout_hbm, gro_hbm,
    gt_hbm, gp_hbm, gi_hbm, gw_hbm,
    tok, sp, win, wout, gro, wrep, disp, comb, dmask, cmask, dlm,
    msg, rcv, msg2, rcv2, xg, act, dh, xht, actt, ys,
    gt_st, gi_st, gw_st, gp, rs, ybuf, zbuf, gbuf,
    in_sems, out_sems, ssem, rsem, ssem2, rsem2, lsems, fsem, frsem, ar_s, ar_r, sem2,
):
    r = lax.axis_index("rep")
    e = lax.axis_index("exp")
    zh = e // 32
    x = (e // 8) % 4
    y = (e // 2) % 4
    c = e % 2

    def device(zhi, zlo, xx, yy, cc):
        return (zlo, zhi * 32 + xx * 8 + yy * 2 + cc)

    def target(i, sign):
        zb = i // 32
        return device(
            (zh + zb) % 2,
            (r + zb) % 2,
            (x + sign * ((i // 8) % 4) + 4) % 4,
            (y + sign * ((i // 2) % 4) + 4) % 4,
            (c + i) % 2,
        )

    loads = [
        pltpu.make_async_copy(src, dst, in_sems.at[n])
        for n, (src, dst) in enumerate(
            ((tok_hbm, tok), (sp_hbm, sp), (gro_hbm, gro), (win_hbm, win), (wout_hbm, wout))
        )
    ]
    for copy in loads:
        copy.start()

    row_group = [ix * 8 + ic for ix in range(4) for ic in range(2) if ix + ic > 0]
    col_group = [zb * 32 + iy * 2 for zb in range(2) for iy in range(4) if zb + iy > 0]
    barrier = pltpu.get_barrier_semaphore()
    for i in row_group + col_group:
        pl.semaphore_signal(barrier, inc=1, device_id=target(i, 1), device_id_type=MESH)
    for dev in (device(zh, 1 - r, x, y, c), device(1 - zh, r, x, y, c)):
        pl.semaphore_signal(barrier, inc=1, device_id=dev, device_id_type=MESH)

    def slot_of(i):
        zb = i // 32
        return (
            ((zh + zb) % 2) * 32
            + ((x + (i // 8) % 4) % 4) * 8
            + ((y + (i // 2) % 4) % 4) * 2
            + (c + i) % 2
        )

    row_i = lax.broadcasted_iota(jnp.int32, (R, S), 0) // B
    pick = (slot_of(row_i) == lax.broadcasted_iota(jnp.int32, (R, S), 1)).astype(F32).astype(BF)
    col_i = lax.broadcasted_iota(jnp.int32, (S, R), 1) // B
    pick_t = (slot_of(col_i) == lax.broadcasted_iota(jnp.int32, (S, R), 0)).astype(F32).astype(BF)
    image = lax.broadcasted_iota(jnp.int32, (R, M), 0) % B

    loads[1].wait()
    wrep[...] = dot_nt(pick, sp[...]).astype(BF)
    loads[0].wait()
    logits = jnp.zeros((R, M), F32)
    for b in range(B):
        logits = jnp.where(image == b, dot_nt(wrep[...], tok[b]), logits)

    top = jnp.max(logits, axis=1, keepdims=True)
    p = jnp.exp(logits - top)
    dispatch = p / jnp.sum(p, axis=1, keepdims=True)
    disp[...] = dispatch
    l3 = logits.reshape(R // 8, 8, M)
    top = jnp.max(l3, axis=0)
    top = jnp.maximum(top, pltpu.roll(top, 4, 0))
    p = jnp.exp(l3 - top[None])
    total = jnp.sum(p, axis=0)
    total = total + pltpu.roll(total, 4, 0)
    combine = (p / total[None]).reshape(R, M)
    comb[...] = combine
    for b in range(B):
        dmask[:, b * M : (b + 1) * M] = jnp.where(image == b, dispatch, 0.0).astype(BF)
        cmask[:, b * M : (b + 1) * M] = jnp.where(image == b, combine, 0.0).astype(BF)
    loads[2].wait()

    def gather_step(p, carry):
        lo = pl.ds(pl.multiple_of(p * 128, 128), 128)
        hi = pl.ds(pl.multiple_of(HALF + p * 128, 128), 128)
        rhs = jnp.concatenate([tok[:, :, lo], tok[:, :, hi]], axis=2).reshape(B * M, 256)
        first = dot(dmask[...], rhs)
        rhs = jnp.concatenate([gro[:, :, lo], gro[:, :, hi]], axis=2).reshape(B * M, 256)
        second = dot(cmask[...], rhs)
        store_message(msg, p, first, second)
        return carry

    lax.fori_loop(0, 5, gather_step, 0)

    pl.semaphore_wait(barrier, 16)
    for i in row_group:
        pl.semaphore_signal(sem2, inc=1, device_id=target(i, 1), device_id_type=MESH)
    pl.semaphore_wait(sem2, 7)

    def send_all(src, dst, ssem, rsem, sign):
        def body(k, carry):
            i = (k * 29) % 64
            pltpu.make_async_remote_copy(
                src_ref=src.at[i],
                dst_ref=dst.at[i],
                send_sem=ssem,
                recv_sem=rsem,
                device_id=target(i, sign),
                device_id_type=MESH,
            ).start()
            return carry

        lax.fori_loop(1, 64, body, 0)

    def wait_63(buf, sem):
        part = buf.at[pl.ds(1, S - 1)]
        pltpu.make_async_copy(part, part, sem).wait()

    send_all(msg, rcv, ssem, rsem, 1)
    own = pltpu.make_async_copy(msg.at[0], rcv.at[0], lsems.at[0])
    own.start()
    loads[3].wait()
    loads[4].wait()
    own.wait()
    wait_63(rcv, rsem)

    def unpack_step(p, carry):
        first, second = load_message(rcv, p)
        for h in range(2):
            at = pl.ds(pl.multiple_of(h * HALF + p * 128, 128), 128)
            xg[0, 0, :, at] = first[:, h * 128 : (h + 1) * 128].astype(BF)
            xg[0, 1, :, at] = second[:, h * 128 : (h + 1) * 128].astype(BF)
        return carry

    lax.fori_loop(0, 5, unpack_step, 0)

    forward = pltpu.make_async_remote_copy(
        src_ref=xg.at[0],
        dst_ref=xg.at[1],
        send_sem=fsem,
        recv_sem=frsem,
        device_id=(1 - r, e),
        device_id_type=MESH,
    )
    forward.start()

    def hidden(side):
        def step(j, carry):
            at = pl.ds(pl.multiple_of(j * 256, 256), 256)
            pre = dot(xg[side, 0], win[:, at])
            d_act = dot_nt(xg[side, 1], wout[at, :])
            value, slope = gelu_both(pre)
            act[side, :, at] = value.astype(BF)
            dh[side, :, at] = (d_act * slope).astype(BF)
            return carry

        lax.fori_loop(0, F // 256, step, 0)

    hidden(0)

    def back_step(p, carry):
        lo = pl.ds(pl.multiple_of(p * 128, 128), 128)
        hi = pl.ds(pl.multiple_of(HALF + p * 128, 128), 128)
        first = dot(act[0], jnp.concatenate([wout[:, lo], wout[:, hi]], axis=1))
        second = dot_nt(dh[0], jnp.concatenate([win[lo, :], win[hi, :]], axis=0))
        store_message(msg2, p, first, second)
        return carry

    lax.fori_loop(0, 5, back_step, 0)
    send_all(msg2, rcv2, ssem2, rsem2, -1)
    own = pltpu.make_async_copy(msg2.at[0], rcv2.at[0], lsems.at[1])
    own.start()

    def grads(side):
        my_cols = pl.ds(pl.multiple_of(r * HALF, 128), HALF)
        my_hidden = pl.ds(pl.multiple_of(r * (F // 2), 256), F // 2)
        xht[...] = xg[side, 0, :, my_cols].T
        actt[...] = act[side, :, my_hidden].T

        def in_step(j, carry):
            at = pl.ds(pl.multiple_of(j * 256, 256), 256)
            term = dot(xht[...], dh[side, :, at])
            if side == 1:
                term = term + gi_st[:, at].astype(F32)
            gi_st[:, at] = term.astype(BF)
            return carry

        lax.fori_loop(0, F // 256, in_step, 0)

        def out_step(j, carry):
            at = pl.ds(pl.multiple_of(j * 256, 256), 256)
            term = dot(actt[...], xg[side, 1, :, at])
            if side == 1:
                term = term + gw_st[:, at].astype(F32)
            gw_st[:, at] = term.astype(BF)
            return carry

        lax.fori_loop(0, D // 256, out_step, 0)

    grads(0)
    own.wait()
    wait_63(rcv2, rsem2)

    def unpack_back(p, carry):
        first, second = load_message(rcv2, p)
        for h in range(2):
            at = pl.ds(pl.multiple_of(h * HALF + p * 128, 128), 128)
            ys[0, :, at] = first[:, h * 128 : (h + 1) * 128].astype(BF)
            ys[1, :, at] = second[:, h * 128 : (h + 1) * 128].astype(BF)
        return carry

    lax.fori_loop(0, 5, unpack_back, 0)

    d_comb = jnp.zeros((R, M), F32)
    d_disp = jnp.zeros((R, M), F32)
    for b in range(B):
        d_comb = jnp.where(image == b, dot_nt(ys[0], gro[b]), d_comb)
        d_disp = jnp.where(image == b, dot_nt(ys[1], tok[b]), d_disp)
    combine = comb[...].reshape(R // 8, 8, M)
    d_comb = d_comb.reshape(R // 8, 8, M)
    total = jnp.sum(combine * d_comb, axis=0)
    total = total + pltpu.roll(total, 4, 0)
    d_logits = (combine * (d_comb - total[None])).reshape(R, M)
    dispatch = disp[...]
    d_logits = d_logits + dispatch * (
        d_disp - jnp.sum(dispatch * d_disp, axis=1, keepdims=True)
    )
    for b in range(B):
        dlm[:, b * M : (b + 1) * M] = jnp.where(image == b, d_logits, 0.0).astype(BF)
    per_slot = dot(pick_t, dlm[...]).astype(BF)

    for j in range(D // 256):
        at = slice(j * 256, (j + 1) * 256)
        rhs = tok[:, :, at].reshape(B * M, 256)
        gp[:, :, at] = dot(per_slot, rhs).reshape(8, 8, 256)

    line = x * 2 + c
    zc = zh * 2 + r

    def line_member(d):
        return device(zh, r, (x + d // 2) % 4, y, (c + d) % 2)

    def line_index(d):
        return ((x + d // 2) % 4) * 2 + (c + d) % 2

    def remote(src, dst, phase, dev):
        return pltpu.make_async_remote_copy(
            src_ref=src,
            dst_ref=dst,
            send_sem=ar_s.at[phase],
            recv_sem=ar_r.at[phase],
            device_id=dev,
            device_id_type=MESH,
        )

    def wait_parts(buf, count, sem):
        part = buf.at[pl.ds(0, count)]
        pltpu.make_async_copy(part, part, sem).wait()

    def tokens_grad(b):
        at = slice(b * M, (b + 1) * M)
        left = jnp.concatenate([dmask[:, at], dlm[:, at]], axis=0).T
        for j in range(D // 256):
            cols = slice(j * 256, (j + 1) * 256)
            right = jnp.concatenate([ys[1, :, cols], wrep[:, cols]], axis=0)
            gt_st[b, :, cols] = dot(left, right).astype(BF)
        copy = pltpu.make_async_copy(gt_st.at[b], gt_hbm.at[b], out_sems.at[b])
        copy.start()
        return copy

    stores = []
    for d in range(1, 8):
        remote(gp.at[line_index(d)], rs.at[line], 0, line_member(d)).start()
    rs[line] = gp[line]
    stores.append(tokens_grad(0))
    stores.append(tokens_grad(1))
    wait_parts(rs, 7, ar_r.at[0])
    ybuf[y] = jnp.sum(rs[...], axis=0)
    for d in range(1, 4):
        remote(ybuf.at[y], ybuf.at[y], 1, device(zh, r, x, (y + d) % 4, c)).start()
    stores.append(tokens_grad(2))
    stores.append(tokens_grad(3))
    wait_parts(ybuf, 3, ar_r.at[1])
    zbuf[zc] = (ybuf[0] + ybuf[1]) + (ybuf[2] + ybuf[3])
    for dh_, dl_ in ((0, 1), (1, 0), (1, 1)):
        dev = device((zh + dh_) % 2, (r + dl_) % 2, x, y, c)
        remote(zbuf.at[zc], zbuf.at[zc], 2, dev).start()

    forward.wait()
    hidden(1)
    wait_parts(zbuf, 3, ar_r.at[2])
    gbuf[line] = (zbuf[0] + zbuf[1]) + (zbuf[2] + zbuf[3])
    for d in range(1, 8):
        remote(gbuf.at[line], gbuf.at[line], 3, line_member(d)).start()
    grads(1)
    for n, (src, dst) in enumerate(((gi_st, gi_hbm), (gw_st, gw_hbm))):
        copy = pltpu.make_async_copy(src, dst, out_sems.at[4 + n])
        copy.start()
        stores.append(copy)
    wait_parts(gbuf, 7, ar_r.at[3])
    copy = pltpu.make_async_copy(gbuf, gp_hbm, out_sems.at[6])
    copy.start()
    stores.append(copy)

    wait_63(msg, ssem)
    wait_63(msg2, ssem2)
    wait_parts(rs, 7, ar_s.at[0])
    wait_parts(ybuf, 3, ar_s.at[1])
    wait_parts(zbuf, 3, ar_s.at[2])
    wait_parts(gbuf, 7, ar_s.at[3])
    for copy in stores:
        copy.wait()


def body(tokens, slot_params, expert_in, expert_out, grad_out):
    vm = pltpu.VMEM
    dma = pltpu.SemaphoreType.DMA
    scratch = [
        vm((B, M, D), BF), vm((D, S), BF), vm((D, F), BF), vm((F, D), BF), vm((B, M, D), BF),
        vm((R, D), BF), vm((R, M), F32), vm((R, M), F32),
        vm((R, B * M), BF), vm((R, B * M), BF), vm((R, B * M), BF),
        vm((S, 16, HALF), BF), vm((S, 16, HALF), BF),
        vm((S, 16, HALF), BF), vm((S, 16, HALF), BF),
        vm((2, 2, R, D), BF), vm((2, R, F), BF), vm((2, R, F), BF),
        vm((HALF, R), BF), vm((F // 2, R), BF), vm((2, R, D), BF),
        vm((B, M, D), BF), vm((HALF, F), BF), vm((F // 2, D), BF),
        vm((8, 8, D), F32), vm((8, 8, D), F32), vm((4, 8, D), F32), vm((4, 8, D), F32),
        vm((8, 8, D), F32),
        dma((5,)), dma((7,)), dma, dma, dma, dma, dma((2,)), dma, dma, dma((4,)), dma((4,)),
        pltpu.SemaphoreType.REGULAR,
    ]
    anywhere = pl.BlockSpec(memory_space=pl.ANY)
    gt, gp, gi, gw = pl.pallas_call(
        kernel,
        out_shape=(
            jax.ShapeDtypeStruct((B, M, D), BF),
            jax.ShapeDtypeStruct((8, 8, D), F32),
            jax.ShapeDtypeStruct((HALF, F), BF),
            jax.ShapeDtypeStruct((F // 2, D), BF),
        ),
        in_specs=[anywhere] * 5,
        out_specs=(anywhere,) * 4,
        scratch_shapes=scratch,
        compiler_params=pltpu.CompilerParams(
            collective_id=0, has_side_effects=True, vmem_limit_bytes=60 << 20
        ),
    )(tokens, slot_params, expert_in[0], expert_out[0], grad_out)
    return gt, gp.reshape(S, D).T, gi[None], gw[None]


def solution(mesh):
    in_specs = (
        P(("rep", "exp"), None, None),
        P(),
        P("exp", None, None),
        P("exp", None, None),
        P(("rep", "exp"), None, None),
    )
    out_specs = (P(("rep", "exp"), None, None), P(), P("exp", "rep", None), P("exp", "rep", None))
    return jax.shard_map(body, mesh=mesh, in_specs=in_specs, out_specs=out_specs, check_vma=False)
```

```python
import math

import jax
import jax.numpy as jnp
from jax import lax
from jax.experimental import pallas as pl
from jax.experimental.pallas import tpu as pltpu
from jax.sharding import PartitionSpec as P

GELU_C = math.sqrt(2.0 / math.pi)
CUBIC = 0.044715
MESH = pl.DeviceIdType.MESH

D = 1280
F = 2560
M = 256
S = 64
HS = S // 2
B = 4
R = S * B
HR = R // 2
HALF = D // 2
BF = jnp.bfloat16
F32 = jnp.float32

NT = (((1,), (1,)), ((), ()))


def dot(a, b):
    return jnp.dot(a, b, preferred_element_type=F32)


def dot_nt(a, b):
    return lax.dot_general(a, b, NT, preferred_element_type=F32)


def by_parity(buf, half):
    return buf.at[pl.ds(half * HS, HS)].reshape(HS // 2, 2, 16, HALF)


def pack(first, second):
    rows, width = first.shape
    a = first.reshape(rows // 8, 8, width)
    g = second.reshape(rows // 8, 8, width)
    low = lax.broadcasted_iota(jnp.int32, a.shape, 1) < 4
    even = jnp.where(low, a, pltpu.roll(g, 4, 1))
    odd = jnp.where(low, pltpu.roll(a, 4, 1), g)
    return even, odd


def unpack(even, odd):
    rows = even.shape[0] * 8
    low = lax.broadcasted_iota(jnp.int32, even.shape, 1) < 4
    a = jnp.where(low, even, pltpu.roll(odd, 4, 1))
    g = jnp.where(low, pltpu.roll(even, 4, 1), odd)
    return a.reshape(rows, -1), g.reshape(rows, -1)


def columns(p):
    return slice(p * 128, (p + 1) * 128), slice(HALF + p * 128, HALF + (p + 1) * 128)


def store_message(msg, half, p, first, second):
    even, odd = pack(first, second)
    msg = by_parity(msg, half)
    for j, v in enumerate((even, odd)):
        rows = jnp.concatenate([v[:, :, :128], v[:, :, 128:]], axis=1)
        msg[:, j, :, columns(p)[0]] = rows.astype(BF)


def load_message(rcv, half, p):
    rcv = by_parity(rcv, half)
    sides = []
    for j in range(2):
        rows = rcv[:, j, :, columns(p)[0]].astype(F32)
        sides.append(jnp.concatenate([rows[:, :8], rows[:, 8:]], axis=2))
    return unpack(sides[0], sides[1])


def gelu_both(v):
    u = v * v
    t = jnp.tanh(GELU_C * (v + CUBIC * v * u))
    half = 0.5 * (1.0 + t)
    slope = half + 0.5 * v * (1.0 - t * t) * (GELU_C * (1.0 + 3.0 * CUBIC * u))
    return half * v, slope


def kernel(
    tok_hbm, sp_hbm, win_hbm, wout_hbm, gro_hbm,
    gt_out, gp_out, gi_out, gw_out,
    tok, sp, win, wout, gro, wrep, disp, comb, dmask, cmask, dlm,
    msg, rcv, msg2, rcv2, xg, act, dh, xht, actt, ys, gp, rs, ybuf, zbuf,
    in_sems, ssem, rsem, ssem2, rsem2, lsems, fsem, frsem, ar_s, ar_r, sem2,
):
    r = lax.axis_index("rep")
    e = lax.axis_index("exp")
    zh = e // 32
    x = (e // 8) % 4
    y = (e // 2) % 4
    c = e % 2

    def device(zhi, zlo, xx, yy, cc):
        return (zlo, zhi * 32 + xx * 8 + yy * 2 + cc)

    def target(i, sign):
        zb = (i // 16) % 2
        return device(
            (zh + zb) % 2,
            (r + zb) % 2,
            (x + sign * ((i // 4) % 4) + 4) % 4,
            (y + sign * (i % 4) + 4) % 4,
            (c + i // 32) % 2,
        )

    loads = [
        pltpu.make_async_copy(src, dst, in_sems.at[n])
        for n, (src, dst) in enumerate(
            ((tok_hbm, tok), (sp_hbm, sp), (gro_hbm, gro), (win_hbm, win), (wout_hbm, wout))
        )
    ]
    for copy in loads:
        copy.start()

    row_group = [ic * 32 + ix * 4 for ic in range(2) for ix in range(4) if ic + ix > 0]
    col_group = [zb * 16 + iy for zb in range(2) for iy in range(4) if zb + iy > 0]
    barrier = pltpu.get_barrier_semaphore()
    for i in row_group + col_group:
        pl.semaphore_signal(barrier, inc=1, device_id=target(i, 1), device_id_type=MESH)
    for dev in (device(zh, 1 - r, x, y, c), device(1 - zh, r, x, y, c)):
        pl.semaphore_signal(barrier, inc=1, device_id=dev, device_id_type=MESH)

    def slot_of(i):
        zb = (i // 16) % 2
        return (
            ((zh + zb) % 2) * 32
            + ((x + (i // 4) % 4) % 4) * 8
            + ((y + i % 4) % 4) * 2
            + (c + i // 32) % 2
        )

    row_i = lax.broadcasted_iota(jnp.int32, (R, S), 0) // B
    pick = (slot_of(row_i) == lax.broadcasted_iota(jnp.int32, (R, S), 1)).astype(F32).astype(BF)
    col_i = lax.broadcasted_iota(jnp.int32, (S, R), 1) // B
    pick_t = (slot_of(col_i) == lax.broadcasted_iota(jnp.int32, (S, R), 0)).astype(F32).astype(BF)
    image = lax.broadcasted_iota(jnp.int32, (R, M), 0) % B

    loads[1].wait()
    wrep[...] = dot(pick, sp[...]).astype(BF)
    loads[0].wait()
    logits = jnp.zeros((R, M), F32)
    for b in range(B):
        logits = jnp.where(image == b, dot_nt(wrep[...], tok[b]), logits)

    top = jnp.max(logits, axis=1, keepdims=True)
    p = jnp.exp(logits - top)
    dispatch = p / jnp.sum(p, axis=1, keepdims=True)
    disp[...] = dispatch
    l3 = logits.reshape(R // 8, 8, M)
    top = jnp.max(l3, axis=0)
    top = jnp.maximum(top, pltpu.roll(top, 4, 0))
    p = jnp.exp(l3 - top[None])
    total = jnp.sum(p, axis=0)
    total = total + pltpu.roll(total, 4, 0)
    combine = (p / total[None]).reshape(R, M)
    comb[...] = combine
    for b in range(B):
        dmask[:, b * M : (b + 1) * M] = jnp.where(image == b, dispatch, 0.0).astype(BF)
        cmask[:, b * M : (b + 1) * M] = jnp.where(image == b, combine, 0.0).astype(BF)
    loads[2].wait()

    pl.semaphore_wait(barrier, 16)
    for i in row_group:
        pl.semaphore_signal(sem2, inc=1, device_id=target(i, 1), device_id_type=MESH)

    def gather(half):
        rows = slice(half * HR, (half + 1) * HR)
        for p in range(5):
            lo, hi = columns(p)
            rhs = jnp.concatenate([tok[:, :, lo], tok[:, :, hi]], axis=2).reshape(B * M, 256)
            first = dot(dmask[rows, :], rhs)
            rhs = jnp.concatenate([gro[:, :, lo], gro[:, :, hi]], axis=2).reshape(B * M, 256)
            second = dot(cmask[rows, :], rhs)
            store_message(msg, half, p, first, second)

    def send_half(half, src, dst, ssem, rsem, sign):
        def body(k, carry):
            i = half * HS + (k * 13) % HS
            pltpu.make_async_remote_copy(
                src_ref=src.at[i],
                dst_ref=dst.at[i],
                send_sem=ssem.at[half],
                recv_sem=rsem.at[half],
                device_id=target(i, sign),
                device_id_type=MESH,
            ).start()
            return carry

        lax.fori_loop(1 - half, HS, body, 0)

    def wait_half(half, buf, sem):
        part = buf.at[pl.ds(half * HS + 1 - half, HS - 1 + half)]
        pltpu.make_async_copy(part, part, sem.at[half]).wait()

    gather(0)
    pl.semaphore_wait(sem2, 7)
    send_half(0, msg, rcv, ssem, rsem, 1)
    own = pltpu.make_async_copy(msg.at[0], rcv.at[0], lsems.at[0])
    own.start()
    gather(1)
    send_half(1, msg, rcv, ssem, rsem, 1)
    loads[3].wait()
    loads[4].wait()
    own.wait()

    def hidden(side, halves):
        rows = slice(halves[0] * HR, (halves[-1] + 1) * HR)
        count = len(halves) * HR
        at_h = slice(halves[0], halves[-1] + 1)
        previous = None
        for j in range(F // 256 + 1):
            current = None
            if j < F // 256:
                at = slice(j * 256, (j + 1) * 256)
                pre = dot(xg[side, at_h, 0].reshape(count, D), win[:, at])
                d_act = dot_nt(xg[side, at_h, 1].reshape(count, D), wout[at, :])
                current = (pre, d_act, at)
            if previous is not None:
                pre, d_act, at = previous
                value, slope = gelu_both(pre)
                act[side, rows, at] = value.astype(BF)
                dh[side, rows, at] = (d_act * slope).astype(BF)
            previous = current

    forwards = []

    def expert(half):
        wait_half(half, rcv, rsem)
        for p in range(5):
            first, second = load_message(rcv, half, p)
            for h, at in enumerate(columns(p)):
                xg[0, half, 0, :, at] = first[:, h * 128 : (h + 1) * 128].astype(BF)
                xg[0, half, 1, :, at] = second[:, h * 128 : (h + 1) * 128].astype(BF)
        forward = pltpu.make_async_remote_copy(
            src_ref=xg.at[0, half],
            dst_ref=xg.at[1, half],
            send_sem=fsem.at[half],
            recv_sem=frsem.at[half],
            device_id=(1 - r, e),
            device_id_type=MESH,
        )
        forward.start()
        forwards.append(forward)
        hidden(0, (half,))
        rows = slice(half * HR, (half + 1) * HR)
        for p in range(5):
            lo, hi = columns(p)
            first = dot(act[0, rows, :], jnp.concatenate([wout[:, lo], wout[:, hi]], axis=1))
            second = dot_nt(dh[0, rows, :], jnp.concatenate([win[lo, :], win[hi, :]], axis=0))
            store_message(msg2, half, p, first, second)
        send_half(half, msg2, rcv2, ssem2, rsem2, -1)

    expert(0)
    own = pltpu.make_async_copy(msg2.at[0], rcv2.at[0], lsems.at[1])
    own.start()
    expert(1)

    my_cols = pl.ds(pl.multiple_of(r * HALF, 128), HALF)
    my_hidden = pl.ds(pl.multiple_of(r * (F // 2), 256), F // 2)

    def grad_in(side):
        xht[...] = xg[side, :, 0, :, my_cols].reshape(R, HALF).T
        for j in range(F // 256):
            at = slice(j * 256, (j + 1) * 256)
            term = dot(xht[...], dh[side, :, at])
            if side == 1:
                term = term + gi_out[:, at].astype(F32)
            gi_out[:, at] = term.astype(BF)

    def grad_out(side):
        actt[...] = act[side, :, my_hidden].T
        for j in range(D // 256):
            at = slice(j * 256, (j + 1) * 256)
            term = dot(actt[...], xg[side, :, 1, :, at].reshape(R, 256))
            if side == 1:
                term = term + gw_out[:, at].astype(F32)
            gw_out[:, at] = term.astype(BF)

    grad_in(0)
    grad_out(0)
    own.wait()
    for half in range(2):
        wait_half(half, rcv2, rsem2)
        rows = slice(half * HR, (half + 1) * HR)
        for p in range(5):
            first, second = load_message(rcv2, half, p)
            for h, at in enumerate(columns(p)):
                ys[0, rows, at] = first[:, h * 128 : (h + 1) * 128].astype(BF)
                ys[1, rows, at] = second[:, h * 128 : (h + 1) * 128].astype(BF)

    d_comb = jnp.zeros((R, M), F32)
    d_disp = jnp.zeros((R, M), F32)
    for b in range(B):
        d_comb = jnp.where(image == b, dot_nt(ys[0], gro[b]), d_comb)
        d_disp = jnp.where(image == b, dot_nt(ys[1], tok[b]), d_disp)
    combine = comb[...].reshape(R // 8, 8, M)
    d_comb = d_comb.reshape(R // 8, 8, M)
    total = jnp.sum(combine * d_comb, axis=0)
    total = total + pltpu.roll(total, 4, 0)
    d_logits = (combine * (d_comb - total[None])).reshape(R, M)
    dispatch = disp[...]
    d_logits = d_logits + dispatch * (
        d_disp - jnp.sum(dispatch * d_disp, axis=1, keepdims=True)
    )
    for b in range(B):
        dlm[:, b * M : (b + 1) * M] = jnp.where(image == b, d_logits, 0.0).astype(BF)
    per_slot = dot(pick_t, dlm[...]).astype(BF)

    for j in range(D // 256):
        at = slice(j * 256, (j + 1) * 256)
        rhs = tok[:, :, at].reshape(B * M, 256)
        gp[:, :, at] = dot(per_slot, rhs).reshape(8, 8, 256)

    line = x * 2 + c
    zc = zh * 2 + r

    def line_member(d):
        return device(zh, r, (x + d // 2) % 4, y, (c + d) % 2)

    def line_index(d):
        return ((x + d // 2) % 4) * 2 + (c + d) % 2

    def remote(src, dst, phase, dev):
        return pltpu.make_async_remote_copy(
            src_ref=src,
            dst_ref=dst,
            send_sem=ar_s.at[phase],
            recv_sem=ar_r.at[phase],
            device_id=dev,
            device_id_type=MESH,
        )

    def wait_parts(buf, count, sem):
        part = buf.at[pl.ds(0, count)]
        pltpu.make_async_copy(part, part, sem).wait()

    def tokens_grad(b):
        at = slice(b * M, (b + 1) * M)
        left = jnp.concatenate([dmask[:, at], dlm[:, at]], axis=0).T
        for j in range(D // 256):
            cols = slice(j * 256, (j + 1) * 256)
            right = jnp.concatenate([ys[1, :, cols], wrep[:, cols]], axis=0)
            gt_out[b, :, cols] = dot(left, right).astype(BF)

    for d in range(1, 8):
        remote(gp.at[line_index(d)], rs.at[line], 0, line_member(d)).start()
    rs[line] = gp[line]
    for forward in forwards:
        forward.wait()
    hidden(1, (0, 1))

    wait_parts(rs, 7, ar_r.at[0])
    ybuf[y] = jnp.sum(rs[...], axis=0)
    for d in range(1, 4):
        remote(ybuf.at[y], ybuf.at[y], 1, device(zh, r, x, (y + d) % 4, c)).start()
    grad_in(1)

    wait_parts(ybuf, 3, ar_r.at[1])
    zbuf[zc] = (ybuf[0] + ybuf[1]) + (ybuf[2] + ybuf[3])
    for dh_, dl_ in ((0, 1), (1, 0), (1, 1)):
        dev = device((zh + dh_) % 2, (r + dl_) % 2, x, y, c)
        remote(zbuf.at[zc], zbuf.at[zc], 2, dev).start()
    grad_out(1)

    wait_parts(zbuf, 3, ar_r.at[2])
    gp_out[line] = (zbuf[0] + zbuf[1]) + (zbuf[2] + zbuf[3])
    for d in range(1, 8):
        remote(gp_out.at[line], gp_out.at[line], 3, line_member(d)).start()
    for b in range(B):
        tokens_grad(b)
    wait_parts(gp_out, 7, ar_r.at[3])

    for half in range(2):
        wait_half(half, msg, ssem)
        wait_half(half, msg2, ssem2)
    wait_parts(rs, 7, ar_s.at[0])
    wait_parts(ybuf, 3, ar_s.at[1])
    wait_parts(zbuf, 3, ar_s.at[2])
    wait_parts(gp_out, 7, ar_s.at[3])


def store_kernel(*refs):
    sources, targets, sems = refs[:4], refs[4:8], refs[8]
    copies = [
        pltpu.make_async_copy(src, dst, sems.at[n])
        for n, (src, dst) in enumerate(zip(sources, targets))
    ]
    for copy in copies:
        copy.start()
    for copy in copies:
        copy.wait()


def body(tokens, slot_params, expert_in, expert_out, grad_out):
    vm = pltpu.VMEM
    dma = pltpu.SemaphoreType.DMA
    scratch = [
        vm((B, M, D), BF), vm((S, D), BF), vm((D, F), BF), vm((F, D), BF), vm((B, M, D), BF),
        vm((R, D), BF), vm((R, M), F32), vm((R, M), F32),
        vm((R, B * M), BF), vm((R, B * M), BF), vm((R, B * M), BF),
        vm((S, 16, HALF), BF), vm((S, 16, HALF), BF),
        vm((S, 16, HALF), BF), vm((S, 16, HALF), BF),
        vm((2, 2, 2, HR, D), BF), vm((2, R, F), BF), vm((2, R, F), BF),
        vm((HALF, R), BF), vm((F // 2, R), BF), vm((2, R, D), BF),
        vm((8, 8, D), F32), vm((8, 8, D), F32), vm((4, 8, D), F32), vm((4, 8, D), F32),
        dma((5,)), dma((2,)), dma((2,)), dma((2,)), dma((2,)), dma((2,)), dma((2,)), dma((2,)),
        dma((4,)), dma((4,)), pltpu.SemaphoreType.REGULAR,
    ]
    anywhere = pl.BlockSpec(memory_space=pl.ANY)
    in_vmem = pl.BlockSpec(memory_space=vm)
    shapes = (((B, M, D), BF), ((8, 8, D), F32), ((HALF, F), BF), ((F // 2, D), BF))
    results = pl.pallas_call(
        kernel,
        out_shape=tuple(vm(*shape) for shape in shapes),
        in_specs=[anywhere] * 5,
        out_specs=(in_vmem,) * 4,
        scratch_shapes=scratch,
        compiler_params=pltpu.CompilerParams(
            collective_id=0, has_side_effects=True, vmem_limit_bytes=48 << 20
        ),
    )(tokens, slot_params.T, expert_in[0], expert_out[0], grad_out)
    gt, gp, gi, gw = pl.pallas_call(
        store_kernel,
        out_shape=tuple(jax.ShapeDtypeStruct(*shape) for shape in shapes),
        in_specs=[in_vmem] * 4,
        out_specs=(anywhere,) * 4,
        scratch_shapes=[dma((4,))],
        compiler_params=pltpu.CompilerParams(vmem_limit_bytes=1 << 20),
    )(*(pltpu.with_memory_space_constraint(v, vm) for v in results))
    return gt, gp.reshape(S, D).T, gi[None], gw[None]


def solution(mesh):
    in_specs = (
        P(("rep", "exp"), None, None),
        P(),
        P("exp", None, None),
        P("exp", None, None),
        P(("rep", "exp"), None, None),
    )
    out_specs = (P(("rep", "exp"), None, None), P(), P("exp", "rep", None), P("exp", "rep", None))
    return jax.shard_map(body, mesh=mesh, in_specs=in_specs, out_specs=out_specs, check_vma=False)
```

```python
import math

import jax
import jax.numpy as jnp
from jax import lax
from jax.experimental import pallas as pl
from jax.experimental.pallas import tpu as pltpu
from jax.sharding import PartitionSpec as P

GELU_C = math.sqrt(2.0 / math.pi)
CUBIC = 0.044715
MESH = pl.DeviceIdType.MESH

D = 1280
F = 2560
M = 256
S = 64
HS = S // 2
B = 4
R = S * B
HR = R // 2
HALF = D // 2
BF = jnp.bfloat16
F32 = jnp.float32

def hops(i):
    return (i // 16) % 2 + (0, 1, 2, 1)[(i // 4) % 4] + (0, 1, 2, 1)[i % 4]


FAR_FIRST = sorted(range(HS), key=lambda i: -hops(i))
PIECE = 384

NT = (((1,), (1,)), ((), ()))


def dot(a, b):
    return jnp.dot(a, b, preferred_element_type=F32)


def dot_nt(a, b):
    return lax.dot_general(a, b, NT, preferred_element_type=F32)


def by_parity(buf, half):
    return buf.at[pl.ds(half * HS, HS)].reshape(HS // 2, 2, 16, HALF)


def pack(first, second):
    rows, width = first.shape
    a = first.reshape(rows // 8, 8, width)
    g = second.reshape(rows // 8, 8, width)
    low = lax.broadcasted_iota(jnp.int32, a.shape, 1) < 4
    even = jnp.where(low, a, pltpu.roll(g, 4, 1))
    odd = jnp.where(low, pltpu.roll(a, 4, 1), g)
    return even, odd


def unpack(even, odd):
    rows = even.shape[0] * 8
    low = lax.broadcasted_iota(jnp.int32, even.shape, 1) < 4
    a = jnp.where(low, even, pltpu.roll(odd, 4, 1))
    g = jnp.where(low, pltpu.roll(even, 4, 1), odd)
    return a.reshape(rows, -1), g.reshape(rows, -1)


def columns(p):
    return slice(p * 128, (p + 1) * 128), slice(HALF + p * 128, HALF + (p + 1) * 128)


def store_message(msg, half, p, first, second):
    even, odd = pack(first, second)
    msg = by_parity(msg, half)
    for j, v in enumerate((even, odd)):
        rows = jnp.concatenate([v[:, :, :128], v[:, :, 128:]], axis=1)
        msg[:, j, :, columns(p)[0]] = rows.astype(BF)


def load_message(rcv, half, p):
    rcv = by_parity(rcv, half)
    sides = []
    for j in range(2):
        rows = rcv[:, j, :, columns(p)[0]].astype(F32)
        sides.append(jnp.concatenate([rows[:, :8], rows[:, 8:]], axis=2))
    return unpack(sides[0], sides[1])


def gelu_both(v):
    u = v * v
    t = jnp.tanh(GELU_C * (v + CUBIC * v * u))
    half = 0.5 * (1.0 + t)
    slope = half + 0.5 * v * (1.0 - t * t) * (GELU_C * (1.0 + 3.0 * CUBIC * u))
    return half * v, slope


def kernel(
    tok_hbm, sp_hbm, win_hbm, wout_hbm, gro_hbm,
    gt_out, gp_out, gi_out, gw_out,
    tok, sp, win, wout, gro, wrep, disp, comb, dmask, cmask, dlm,
    msg, rcv, msg2, rcv2, xg, act, dh, xht, actt, ys, gp, cbuf, mine, rs, zbuf, whole,
    in_sems, ssem, rsem, ssem2, rsem2, lsems, fsem, frsem, ar_s, ar_r, sem2,
):
    r = lax.axis_index("rep")
    e = lax.axis_index("exp")
    zh = e // 32
    x = (e // 8) % 4
    y = (e // 2) % 4
    c = e % 2

    def device(zhi, zlo, xx, yy, cc):
        return (zlo, zhi * 32 + xx * 8 + yy * 2 + cc)

    def target(i, sign):
        zb = (i // 16) % 2
        return device(
            (zh + zb) % 2,
            (r + zb) % 2,
            (x + sign * ((i // 4) % 4) + 4) % 4,
            (y + sign * (i % 4) + 4) % 4,
            (c + i // 32) % 2,
        )

    loads = [
        pltpu.make_async_copy(src, dst, in_sems.at[n])
        for n, (src, dst) in enumerate(
            ((tok_hbm, tok), (sp_hbm, sp), (gro_hbm, gro), (win_hbm, win), (wout_hbm, wout))
        )
    ]
    for copy in loads:
        copy.start()

    row_group = [ic * 32 + ix * 4 for ic in range(2) for ix in range(4) if ic + ix > 0]
    col_group = [zb * 16 + iy for zb in range(2) for iy in range(4) if zb + iy > 0]
    barrier = pltpu.get_barrier_semaphore()
    for i in row_group + col_group:
        pl.semaphore_signal(barrier, inc=1, device_id=target(i, 1), device_id_type=MESH)
    for dev in (device(zh, 1 - r, x, y, c), device(1 - zh, r, x, y, c)):
        pl.semaphore_signal(barrier, inc=1, device_id=dev, device_id_type=MESH)

    def slot_of(i):
        zb = (i // 16) % 2
        return (
            ((zh + zb) % 2) * 32
            + ((x + (i // 4) % 4) % 4) * 8
            + ((y + i % 4) % 4) * 2
            + (c + i // 32) % 2
        )

    row_i = lax.broadcasted_iota(jnp.int32, (R, S), 0) // B
    pick = (slot_of(row_i) == lax.broadcasted_iota(jnp.int32, (R, S), 1)).astype(F32).astype(BF)
    col_i = lax.broadcasted_iota(jnp.int32, (S, R), 1) // B
    pick_t = (slot_of(col_i) == lax.broadcasted_iota(jnp.int32, (S, R), 0)).astype(F32).astype(BF)
    image = lax.broadcasted_iota(jnp.int32, (R, M), 0) % B

    loads[1].wait()
    wrep[...] = dot(pick, sp[...]).astype(BF)
    loads[0].wait()
    logits = jnp.zeros((R, M), F32)
    for b in range(B):
        logits = jnp.where(image == b, dot_nt(wrep[...], tok[b]), logits)

    top = jnp.max(logits, axis=1, keepdims=True)
    p = jnp.exp(logits - top)
    dispatch = p / jnp.sum(p, axis=1, keepdims=True)
    disp[...] = dispatch
    l3 = logits.reshape(R // 8, 8, M)
    top = jnp.max(l3, axis=0)
    top = jnp.maximum(top, pltpu.roll(top, 4, 0))
    p = jnp.exp(l3 - top[None])
    total = jnp.sum(p, axis=0)
    total = total + pltpu.roll(total, 4, 0)
    combine = (p / total[None]).reshape(R, M)
    comb[...] = combine
    for b in range(B):
        dmask[:, b * M : (b + 1) * M] = jnp.where(image == b, dispatch, 0.0).astype(BF)
        cmask[:, b * M : (b + 1) * M] = jnp.where(image == b, combine, 0.0).astype(BF)
    loads[2].wait()

    pl.semaphore_wait(barrier, 16)
    for i in row_group:
        pl.semaphore_signal(sem2, inc=1, device_id=target(i, 1), device_id_type=MESH)

    def gather(half):
        rows = slice(half * HR, (half + 1) * HR)
        for p in range(5):
            lo, hi = columns(p)
            rhs = jnp.concatenate([tok[:, :, lo], tok[:, :, hi]], axis=2).reshape(B * M, 256)
            first = dot(dmask[rows, :], rhs)
            rhs = jnp.concatenate([gro[:, :, lo], gro[:, :, hi]], axis=2).reshape(B * M, 256)
            second = dot(cmask[rows, :], rhs)
            store_message(msg, half, p, first, second)

    def send_half(half, src, dst, ssem, rsem, sign):
        for k in FAR_FIRST:
            i = half * HS + k
            if i > 0:
                pltpu.make_async_remote_copy(
                    src_ref=src.at[i],
                    dst_ref=dst.at[i],
                    send_sem=ssem.at[half],
                    recv_sem=rsem.at[half],
                    device_id=target(i, sign),
                    device_id_type=MESH,
                ).start()

    def wait_half(half, buf, sem):
        part = buf.at[pl.ds(half * HS + 1 - half, HS - 1 + half)]
        pltpu.make_async_copy(part, part, sem.at[half]).wait()

    gather(0)
    pl.semaphore_wait(sem2, 7)
    send_half(0, msg, rcv, ssem, rsem, 1)
    own = pltpu.make_async_copy(msg.at[0], rcv.at[0], lsems.at[0])
    own.start()
    gather(1)
    send_half(1, msg, rcv, ssem, rsem, 1)
    loads[3].wait()
    loads[4].wait()
    own.wait()

    def hidden(side, halves):
        rows = slice(halves[0] * HR, (halves[-1] + 1) * HR)
        count = len(halves) * HR
        at_h = slice(halves[0], halves[-1] + 1)
        previous = None
        for j in range(F // 256 + 1):
            current = None
            if j < F // 256:
                at = slice(j * 256, (j + 1) * 256)
                pre = dot(xg[side, at_h, 0].reshape(count, D), win[:, at])
                d_act = dot_nt(xg[side, at_h, 1].reshape(count, D), wout[at, :])
                current = (pre, d_act, at)
            if previous is not None:
                pre, d_act, at = previous
                value, slope = gelu_both(pre)
                act[side, rows, at] = value.astype(BF)
                dh[side, rows, at] = (d_act * slope).astype(BF)
            previous = current

    forwards = []

    def expert(half):
        wait_half(half, rcv, rsem)
        for p in range(5):
            first, second = load_message(rcv, half, p)
            for h, at in enumerate(columns(p)):
                xg[0, half, 0, :, at] = first[:, h * 128 : (h + 1) * 128].astype(BF)
                xg[0, half, 1, :, at] = second[:, h * 128 : (h + 1) * 128].astype(BF)
        forward = pltpu.make_async_remote_copy(
            src_ref=xg.at[0, half],
            dst_ref=xg.at[1, half],
            send_sem=fsem.at[half],
            recv_sem=frsem.at[half],
            device_id=(1 - r, e),
            device_id_type=MESH,
        )
        forward.start()
        forwards.append(forward)
        hidden(0, (half,))
        rows = slice(half * HR, (half + 1) * HR)
        for p in range(5):
            lo, hi = columns(p)
            first = dot(act[0, rows, :], jnp.concatenate([wout[:, lo], wout[:, hi]], axis=1))
            second = dot_nt(dh[0, rows, :], jnp.concatenate([win[lo, :], win[hi, :]], axis=0))
            store_message(msg2, half, p, first, second)
        send_half(half, msg2, rcv2, ssem2, rsem2, -1)

    expert(0)
    own = pltpu.make_async_copy(msg2.at[0], rcv2.at[0], lsems.at[1])
    own.start()
    expert(1)

    my_cols = pl.ds(pl.multiple_of(r * HALF, 128), HALF)
    my_hidden = pl.ds(pl.multiple_of(r * (F // 2), 256), F // 2)

    def grad_in(side):
        xht[...] = xg[side, :, 0, :, my_cols].reshape(R, HALF).T
        for j in range(F // 256):
            at = slice(j * 256, (j + 1) * 256)
            term = dot(xht[...], dh[side, :, at])
            if side == 1:
                term = term + gi_out[:, at].astype(F32)
            gi_out[:, at] = term.astype(BF)

    def grad_out(side):
        actt[...] = act[side, :, my_hidden].T
        for j in range(D // 256):
            at = slice(j * 256, (j + 1) * 256)
            term = dot(actt[...], xg[side, :, 1, :, at].reshape(R, 256))
            if side == 1:
                term = term + gw_out[:, at].astype(F32)
            gw_out[:, at] = term.astype(BF)

    grad_in(0)
    grad_out(0)
    own.wait()
    d_comb, d_disp = [], []
    for half in range(2):
        wait_half(half, rcv2, rsem2)
        rows = slice(half * HR, (half + 1) * HR)
        for p in range(5):
            first, second = load_message(rcv2, half, p)
            for h, at in enumerate(columns(p)):
                ys[0, rows, at] = first[:, h * 128 : (h + 1) * 128].astype(BF)
                ys[1, rows, at] = second[:, h * 128 : (h + 1) * 128].astype(BF)
        of_comb = jnp.zeros((HR, M), F32)
        of_disp = jnp.zeros((HR, M), F32)
        for b in range(B):
            of_comb = jnp.where(image[:HR] == b, dot_nt(ys[0, rows, :], gro[b]), of_comb)
            of_disp = jnp.where(image[:HR] == b, dot_nt(ys[1, rows, :], tok[b]), of_disp)
        d_comb.append(of_comb)
        d_disp.append(of_disp)
    d_comb = jnp.concatenate(d_comb, axis=0)
    d_disp = jnp.concatenate(d_disp, axis=0)
    combine = comb[...].reshape(R // 8, 8, M)
    d_comb = d_comb.reshape(R // 8, 8, M)
    total = jnp.sum(combine * d_comb, axis=0)
    total = total + pltpu.roll(total, 4, 0)
    d_logits = (combine * (d_comb - total[None])).reshape(R, M)
    dispatch = disp[...]
    d_logits = d_logits + dispatch * (
        d_disp - jnp.sum(dispatch * d_disp, axis=1, keepdims=True)
    )
    for b in range(B):
        dlm[:, b * M : (b + 1) * M] = jnp.where(image == b, d_logits, 0.0).astype(BF)
    per_slot = dot(pick_t, dlm[...]).astype(BF)

    for q in range(4):
        width = min(PIECE, D - q * PIECE)
        rhs = tok[:, :, q * PIECE : q * PIECE + width].reshape(B * M, width)
        gp[:, :, q, :, :width] = dot(per_slot, rhs).reshape(2, 4, 8, width)
    gp[:, :, 3, :, width:] = jnp.zeros((2, 4, 8, PIECE - width), F32)

    zc = zh * 2 + r
    sibling = device(zh, r, x, y, 1 - c)

    def plane(d):
        xx, yy = (x + d // 4) % 4, (y + d % 4) % 4
        return xx, yy, device(zh, r, xx, yy, c)

    plane_far = sorted(range(1, 16), key=lambda d: -hops(d))

    def remote(src, dst, phase, dev):
        return pltpu.make_async_remote_copy(
            src_ref=src,
            dst_ref=dst,
            send_sem=ar_s.at[phase],
            recv_sem=ar_r.at[phase],
            device_id=dev,
            device_id_type=MESH,
        )

    def wait_parts(buf, count, sem):
        part = buf.at[pl.ds(0, count)]
        pltpu.make_async_copy(part, part, sem).wait()

    def tokens_grad(b):
        at = slice(b * M, (b + 1) * M)
        left = jnp.concatenate([dmask[:, at], dlm[:, at]], axis=0).T
        for j in range(D // 256):
            cols = slice(j * 256, (j + 1) * 256)
            right = jnp.concatenate([ys[1, :, cols], wrep[:, cols]], axis=0)
            gt_out[b, :, cols] = dot(left, right).astype(BF)

    to_core = remote(gp.at[1 - c], cbuf, 0, sibling)
    to_core.start()
    to_core.wait_recv()
    mine[...] = gp[c] + cbuf[...]
    for d in plane_far:
        xx, yy, dev = plane(d)
        remote(mine.at[xx, yy], rs.at[x * 4 + y], 1, dev).start()
    rs[x * 4 + y] = mine[x, y]
    for forward in forwards:
        forward.wait()
    hidden(1, (0, 1))

    wait_parts(rs, 15, ar_r.at[1])
    zbuf[zc] = jnp.sum(rs[...], axis=0)
    for dh_, dl_ in ((0, 1), (1, 0), (1, 1)):
        dev = device((zh + dh_) % 2, (r + dl_) % 2, x, y, c)
        remote(zbuf.at[zc], zbuf.at[zc], 2, dev).start()
    grad_in(1)
    grad_out(1)

    wait_parts(zbuf, 3, ar_r.at[2])
    total = (zbuf[0] + zbuf[1]) + (zbuf[2] + zbuf[3])
    tall = [total[:, t * 128 : (t + 1) * 128] for t in range(3)] + [jnp.zeros((8, 128), F32)]
    me = c * 16 + x * 4 + y
    whole[me] = jnp.concatenate(tall, axis=0).astype(BF)
    for d in sorted(range(1, 32), key=lambda d: -hops(d % 16)):
        xx, yy, cc = (x + (d // 4) % 4) % 4, (y + d % 4) % 4, (c + d // 16) % 2
        remote(whole.at[me], whole.at[me], 3, device(zh, r, xx, yy, cc)).start()
    for b in range(B):
        tokens_grad(b)
    wait_parts(whole, 31, ar_r.at[3])
    for ch in range(2):
        for xy in range(16):
            piece = whole[ch * 16 + xy].astype(F32)
            for t in range(3):
                lane = (xy % 4) * PIECE + t * 128
                if lane < D:
                    gp_out[ch * 4 + xy // 4, :, lane : lane + 128] = piece[t * 8 : t * 8 + 8]

    for half in range(2):
        wait_half(half, msg, ssem)
        wait_half(half, msg2, ssem2)
    to_core.wait_send()
    wait_parts(rs, 15, ar_s.at[1])
    wait_parts(zbuf, 3, ar_s.at[2])
    wait_parts(whole, 31, ar_s.at[3])


def store_kernel(*refs):
    sources, targets, sems = refs[:4], refs[4:8], refs[8]
    copies = []
    for src, dst in zip(sources, targets):
        if len(src.shape) == 3:
            step = 1 if src.shape[0] == B else src.shape[0]
            parts = [pl.ds(n, step) for n in range(0, src.shape[0], step)]
        else:
            parts = [pl.ds(n, 160) for n in range(0, src.shape[0], 160)]
        for part in parts:
            copies.append(pltpu.make_async_copy(src.at[part], dst.at[part], sems.at[len(copies)]))
    for copy in copies:
        copy.start()
    for copy in copies:
        copy.wait()


def body(tokens, slot_params, expert_in, expert_out, grad_out):
    vm = pltpu.VMEM
    dma = pltpu.SemaphoreType.DMA
    scratch = [
        vm((B, M, D), BF), vm((S, D), BF), vm((D, F), BF), vm((F, D), BF), vm((B, M, D), BF),
        vm((R, D), BF), vm((R, M), F32), vm((R, M), F32),
        vm((R, B * M), BF), vm((R, B * M), BF), vm((R, B * M), BF),
        vm((S, 16, HALF), BF), vm((S, 16, HALF), BF),
        vm((S, 16, HALF), BF), vm((S, 16, HALF), BF),
        vm((2, 2, 2, HR, D), BF), vm((2, R, F), BF), vm((2, R, F), BF),
        vm((HALF, R), BF), vm((F // 2, R), BF), vm((2, R, D), BF),
        vm((2, 4, 4, 8, PIECE), F32), vm((4, 4, 8, PIECE), F32), vm((4, 4, 8, PIECE), F32),
        vm((16, 8, PIECE), F32), vm((4, 8, PIECE), F32), vm((32, 32, 128), BF),
        dma((5,)), dma((2,)), dma((2,)), dma((2,)), dma((2,)), dma((2,)), dma((2,)), dma((2,)),
        dma((4,)), dma((4,)), pltpu.SemaphoreType.REGULAR,
    ]
    anywhere = pl.BlockSpec(memory_space=pl.ANY)
    in_vmem = pl.BlockSpec(memory_space=vm)
    shapes = (((B, M, D), BF), ((8, 8, D), F32), ((HALF, F), BF), ((F // 2, D), BF))
    results = pl.pallas_call(
        kernel,
        out_shape=tuple(vm(*shape) for shape in shapes),
        in_specs=[anywhere] * 5,
        out_specs=(in_vmem,) * 4,
        scratch_shapes=scratch,
        compiler_params=pltpu.CompilerParams(
            collective_id=0, has_side_effects=True, vmem_limit_bytes=48 << 20
        ),
    )(tokens, slot_params.T, expert_in[0], expert_out[0], grad_out)
    gt, gp, gi, gw = pl.pallas_call(
        store_kernel,
        out_shape=tuple(jax.ShapeDtypeStruct(*shape) for shape in shapes),
        in_specs=[in_vmem] * 4,
        out_specs=(anywhere,) * 4,
        scratch_shapes=[dma((17,))],
        compiler_params=pltpu.CompilerParams(vmem_limit_bytes=1 << 20),
    )(*(pltpu.with_memory_space_constraint(v, vm) for v in results))
    return gt, gp.reshape(S, D).T, gi[None], gw[None]


def solution(mesh):
    in_specs = (
        P(("rep", "exp"), None, None),
        P(),
        P("exp", None, None),
        P("exp", None, None),
        P(("rep", "exp"), None, None),
    )
    out_specs = (P(("rep", "exp"), None, None), P(), P("exp", "rep", None), P("exp", "rep", None))
    return jax.shard_map(body, mesh=mesh, in_specs=in_specs, out_specs=out_specs, check_vma=False)
```

```python
import math

import jax
import jax.numpy as jnp
from jax import lax
from jax.experimental import pallas as pl
from jax.experimental.pallas import tpu as pltpu
from jax.sharding import PartitionSpec as P

GELU_C = math.sqrt(2.0 / math.pi)
CUBIC = 0.044715
MESH = pl.DeviceIdType.MESH

D = 1280
F = 2560
M = 256
S = 64
HS = S // 2
B = 4
R = S * B
HR = R // 2
HALF = D // 2
BF = jnp.bfloat16
F32 = jnp.float32

def hops(i):
    return (i // 16) % 2 + (0, 1, 2, 1)[(i // 4) % 4] + (0, 1, 2, 1)[i % 4]


FAR_FIRST = sorted(range(HS), key=lambda i: -hops(i))
PIECE = 384

NT = (((1,), (1,)), ((), ()))


def dot(a, b):
    return jnp.dot(a, b, preferred_element_type=F32)


def dot_nt(a, b):
    return lax.dot_general(a, b, NT, preferred_element_type=F32)


def by_parity(buf, half):
    return buf.at[pl.ds(half * HS, HS)].reshape(HS // 2, 2, 16, HALF)


def pack(first, second):
    rows, width = first.shape
    a = first.reshape(rows // 8, 8, width)
    g = second.reshape(rows // 8, 8, width)
    low = lax.broadcasted_iota(jnp.int32, a.shape, 1) < 4
    even = jnp.where(low, a, pltpu.roll(g, 4, 1))
    odd = jnp.where(low, pltpu.roll(a, 4, 1), g)
    return even, odd


def unpack(even, odd):
    rows = even.shape[0] * 8
    low = lax.broadcasted_iota(jnp.int32, even.shape, 1) < 4
    a = jnp.where(low, even, pltpu.roll(odd, 4, 1))
    g = jnp.where(low, pltpu.roll(even, 4, 1), odd)
    return a.reshape(rows, -1), g.reshape(rows, -1)


def columns(p):
    return slice(p * 128, (p + 1) * 128), slice(HALF + p * 128, HALF + (p + 1) * 128)


def store_message(msg, half, p, first, second):
    even, odd = pack(first, second)
    msg = by_parity(msg, half)
    for j, v in enumerate((even, odd)):
        rows = jnp.concatenate([v[:, :, :128], v[:, :, 128:]], axis=1)
        msg[:, j, :, columns(p)[0]] = rows.astype(BF)


def load_message(rcv, half, p):
    rcv = by_parity(rcv, half)
    sides = []
    for j in range(2):
        rows = rcv[:, j, :, columns(p)[0]].astype(F32)
        sides.append(jnp.concatenate([rows[:, :8], rows[:, 8:]], axis=2))
    return unpack(sides[0], sides[1])


def gelu_both(v):
    u = v * v
    t = jnp.tanh(GELU_C * (v + CUBIC * v * u))
    half = 0.5 * (1.0 + t)
    slope = half + 0.5 * v * (1.0 - t * t) * (GELU_C * (1.0 + 3.0 * CUBIC * u))
    return half * v, slope


def kernel(
    tok_hbm, sp_hbm, win_hbm, wout_hbm, gro_hbm,
    gt_out, gp_out, gi_out, gw_out,
    tok, sp, win, wout, gro, wrep, disp, comb, dmask, cmask, dlm,
    msg, rcv, msg2, rcv2, xg, act, dh, xht, actt, ys, gp, cbuf, mine, rs, zbuf, whole,
    in_sems, ssem, rsem, ssem2, rsem2, lsems, fsem, frsem, ar_s, ar_r, sem2,
):
    r = lax.axis_index("rep")
    e = lax.axis_index("exp")
    zh = e // 32
    x = (e // 8) % 4
    y = (e // 2) % 4
    c = e % 2

    def device(zhi, zlo, xx, yy, cc):
        return (zlo, zhi * 32 + xx * 8 + yy * 2 + cc)

    def target(i, sign):
        zb = (i // 16) % 2
        return device(
            (zh + zb) % 2,
            (r + zb) % 2,
            (x + sign * ((i // 4) % 4) + 4) % 4,
            (y + sign * (i % 4) + 4) % 4,
            (c + i // 32) % 2,
        )

    loads = [
        pltpu.make_async_copy(src, dst, in_sems.at[n])
        for n, (src, dst) in enumerate(
            ((tok_hbm, tok), (sp_hbm, sp), (gro_hbm, gro), (win_hbm, win), (wout_hbm, wout))
        )
    ]
    for copy in loads[:3]:
        copy.start()

    row_group = [ic * 32 + ix * 4 for ic in range(2) for ix in range(4) if ic + ix > 0]
    col_group = [zb * 16 + iy for zb in range(2) for iy in range(4) if zb + iy > 0]
    barrier = pltpu.get_barrier_semaphore()
    for i in row_group + col_group:
        pl.semaphore_signal(barrier, inc=1, device_id=target(i, 1), device_id_type=MESH)
    for dev in (device(zh, 1 - r, x, y, c), device(1 - zh, r, x, y, c)):
        pl.semaphore_signal(barrier, inc=1, device_id=dev, device_id_type=MESH)

    def slot_of(i):
        zb = (i // 16) % 2
        return (
            ((zh + zb) % 2) * 32
            + ((x + (i // 4) % 4) % 4) * 8
            + ((y + i % 4) % 4) * 2
            + (c + i // 32) % 2
        )

    row_i = lax.broadcasted_iota(jnp.int32, (R, S), 0) // B
    pick = (slot_of(row_i) == lax.broadcasted_iota(jnp.int32, (R, S), 1)).astype(F32).astype(BF)
    col_i = lax.broadcasted_iota(jnp.int32, (S, R), 1) // B
    pick_t = (slot_of(col_i) == lax.broadcasted_iota(jnp.int32, (S, R), 0)).astype(F32).astype(BF)
    image = lax.broadcasted_iota(jnp.int32, (R, M), 0) % B

    loads[1].wait()
    wrep[...] = dot(pick, sp[...]).astype(BF)
    loads[0].wait()
    logits = jnp.zeros((R, M), F32)
    for b in range(B):
        logits = jnp.where(image == b, dot_nt(wrep[...], tok[b]), logits)

    top = jnp.max(logits, axis=1, keepdims=True)
    p = jnp.exp(logits - top)
    dispatch = p / jnp.sum(p, axis=1, keepdims=True)
    disp[...] = dispatch
    l3 = logits.reshape(R // 8, 8, M)
    top = jnp.max(l3, axis=0)
    top = jnp.maximum(top, pltpu.roll(top, 4, 0))
    p = jnp.exp(l3 - top[None])
    total = jnp.sum(p, axis=0)
    total = total + pltpu.roll(total, 4, 0)
    combine = (p / total[None]).reshape(R, M)
    comb[...] = combine
    for b in range(B):
        dmask[:, b * M : (b + 1) * M] = jnp.where(image == b, dispatch, 0.0).astype(BF)
        cmask[:, b * M : (b + 1) * M] = jnp.where(image == b, combine, 0.0).astype(BF)
    loads[2].wait()
    for copy in loads[3:]:
        copy.start()

    pl.semaphore_wait(barrier, 16)
    for i in row_group:
        pl.semaphore_signal(sem2, inc=1, device_id=target(i, 1), device_id_type=MESH)

    def gather(half):
        rows = slice(half * HR, (half + 1) * HR)
        for p in range(5):
            lo, hi = columns(p)
            rhs = jnp.concatenate([tok[:, :, lo], tok[:, :, hi]], axis=2).reshape(B * M, 256)
            first = dot(dmask[rows, :], rhs)
            rhs = jnp.concatenate([gro[:, :, lo], gro[:, :, hi]], axis=2).reshape(B * M, 256)
            second = dot(cmask[rows, :], rhs)
            store_message(msg, half, p, first, second)

    def send_half(half, src, dst, ssem, rsem, sign):
        for k in FAR_FIRST:
            i = half * HS + k
            if i > 0:
                pltpu.make_async_remote_copy(
                    src_ref=src.at[i],
                    dst_ref=dst.at[i],
                    send_sem=ssem.at[half],
                    recv_sem=rsem.at[half],
                    device_id=target(i, sign),
                    device_id_type=MESH,
                ).start()

    def wait_half(half, buf, sem):
        part = buf.at[pl.ds(half * HS + 1 - half, HS - 1 + half)]
        pltpu.make_async_copy(part, part, sem.at[half]).wait()

    gather(0)
    pl.semaphore_wait(sem2, 7)
    send_half(0, msg, rcv, ssem, rsem, 1)
    own = pltpu.make_async_copy(msg.at[0], rcv.at[0], lsems.at[0])
    own.start()
    gather(1)
    send_half(1, msg, rcv, ssem, rsem, 1)
    loads[3].wait()
    loads[4].wait()
    own.wait()

    def hidden(side, halves):
        rows = slice(halves[0] * HR, (halves[-1] + 1) * HR)
        count = len(halves) * HR
        at_h = slice(halves[0], halves[-1] + 1)
        previous = None
        for j in range(F // 256 + 1):
            current = None
            if j < F // 256:
                at = slice(j * 256, (j + 1) * 256)
                pre = dot(xg[side, at_h, 0].reshape(count, D), win[:, at])
                d_act = dot_nt(xg[side, at_h, 1].reshape(count, D), wout[at, :])
                current = (pre, d_act, at)
            if previous is not None:
                pre, d_act, at = previous
                value, slope = gelu_both(pre)
                act[side, rows, at] = value.astype(BF)
                dh[side, rows, at] = (d_act * slope).astype(BF)
            previous = current

    forwards = []

    def expert(half):
        wait_half(half, rcv, rsem)
        for p in range(5):
            first, second = load_message(rcv, half, p)
            for h, at in enumerate(columns(p)):
                xg[0, half, 0, :, at] = first[:, h * 128 : (h + 1) * 128].astype(BF)
                xg[0, half, 1, :, at] = second[:, h * 128 : (h + 1) * 128].astype(BF)
        forward = pltpu.make_async_remote_copy(
            src_ref=xg.at[0, half],
            dst_ref=xg.at[1, half],
            send_sem=fsem.at[half],
            recv_sem=frsem.at[half],
            device_id=(1 - r, e),
            device_id_type=MESH,
        )
        forward.start()
        forwards.append(forward)
        hidden(0, (half,))
        rows = slice(half * HR, (half + 1) * HR)
        for p in range(5):
            lo, hi = columns(p)
            first = dot(act[0, rows, :], jnp.concatenate([wout[:, lo], wout[:, hi]], axis=1))
            second = dot_nt(dh[0, rows, :], jnp.concatenate([win[lo, :], win[hi, :]], axis=0))
            store_message(msg2, half, p, first, second)
        send_half(half, msg2, rcv2, ssem2, rsem2, -1)

    expert(0)
    own = pltpu.make_async_copy(msg2.at[0], rcv2.at[0], lsems.at[1])
    own.start()
    expert(1)

    my_cols = pl.ds(pl.multiple_of(r * HALF, 128), HALF)
    my_hidden = pl.ds(pl.multiple_of(r * (F // 2), 256), F // 2)

    def grad_in(side):
        xht[...] = xg[side, :, 0, :, my_cols].reshape(R, HALF).T
        for j in range(F // 256):
            at = slice(j * 256, (j + 1) * 256)
            term = dot(xht[...], dh[side, :, at])
            if side == 1:
                term = term + gi_out[:, at].astype(F32)
            gi_out[:, at] = term.astype(BF)

    def grad_out(side):
        actt[...] = act[side, :, my_hidden].T
        for j in range(D // 256):
            at = slice(j * 256, (j + 1) * 256)
            term = dot(actt[...], xg[side, :, 1, :, at].reshape(R, 256))
            if side == 1:
                term = term + gw_out[:, at].astype(F32)
            gw_out[:, at] = term.astype(BF)

    grad_in(0)
    grad_out(0)
    own.wait()
    d_comb, d_disp = [], []
    for half in range(2):
        wait_half(half, rcv2, rsem2)
        rows = slice(half * HR, (half + 1) * HR)
        for p in range(5):
            first, second = load_message(rcv2, half, p)
            for h, at in enumerate(columns(p)):
                ys[0, rows, at] = first[:, h * 128 : (h + 1) * 128].astype(BF)
                ys[1, rows, at] = second[:, h * 128 : (h + 1) * 128].astype(BF)
        of_comb = jnp.zeros((HR, M), F32)
        of_disp = jnp.zeros((HR, M), F32)
        for b in range(B):
            of_comb = jnp.where(image[:HR] == b, dot_nt(ys[0, rows, :], gro[b]), of_comb)
            of_disp = jnp.where(image[:HR] == b, dot_nt(ys[1, rows, :], tok[b]), of_disp)
        d_comb.append(of_comb)
        d_disp.append(of_disp)
    d_comb = jnp.concatenate(d_comb, axis=0)
    d_disp = jnp.concatenate(d_disp, axis=0)
    combine = comb[...].reshape(R // 8, 8, M)
    d_comb = d_comb.reshape(R // 8, 8, M)
    total = jnp.sum(combine * d_comb, axis=0)
    total = total + pltpu.roll(total, 4, 0)
    d_logits = (combine * (d_comb - total[None])).reshape(R, M)
    dispatch = disp[...]
    d_logits = d_logits + dispatch * (
        d_disp - jnp.sum(dispatch * d_disp, axis=1, keepdims=True)
    )
    for b in range(B):
        dlm[:, b * M : (b + 1) * M] = jnp.where(image == b, d_logits, 0.0).astype(BF)
    per_slot = dot(pick_t, dlm[...]).astype(BF)

    for q in range(4):
        width = min(PIECE, D - q * PIECE)
        rhs = tok[:, :, q * PIECE : q * PIECE + width].reshape(B * M, width)
        gp[:, :, q, :, :width] = dot(per_slot, rhs).reshape(2, 4, 8, width)
    gp[:, :, 3, :, width:] = jnp.zeros((2, 4, 8, PIECE - width), F32)

    zc = zh * 2 + r
    sibling = device(zh, r, x, y, 1 - c)

    def plane(d):
        xx, yy = (x + d // 4) % 4, (y + d % 4) % 4
        return xx, yy, device(zh, r, xx, yy, c)

    plane_far = sorted(range(1, 16), key=lambda d: -hops(d))

    def remote(src, dst, phase, dev):
        return pltpu.make_async_remote_copy(
            src_ref=src,
            dst_ref=dst,
            send_sem=ar_s.at[phase],
            recv_sem=ar_r.at[phase],
            device_id=dev,
            device_id_type=MESH,
        )

    def wait_parts(buf, count, sem):
        part = buf.at[pl.ds(0, count)]
        pltpu.make_async_copy(part, part, sem).wait()

    def tokens_grad(b):
        at = slice(b * M, (b + 1) * M)
        left = jnp.concatenate([dmask[:, at], dlm[:, at]], axis=0).T
        for j in range(D // 256):
            cols = slice(j * 256, (j + 1) * 256)
            right = jnp.concatenate([ys[1, :, cols], wrep[:, cols]], axis=0)
            gt_out[b, :, cols] = dot(left, right).astype(BF)

    to_core = remote(gp.at[1 - c], cbuf, 0, sibling)
    to_core.start()
    to_core.wait_recv()
    mine[...] = gp[c] + cbuf[...]
    for d in plane_far:
        xx, yy, dev = plane(d)
        remote(mine.at[xx, yy], rs.at[x * 4 + y], 1, dev).start()
    rs[x * 4 + y] = mine[x, y]
    for forward in forwards:
        forward.wait()
    hidden(1, (0, 1))

    wait_parts(rs, 15, ar_r.at[1])
    zbuf[zc] = jnp.sum(rs[...], axis=0)
    for dh_, dl_ in ((0, 1), (1, 0), (1, 1)):
        dev = device((zh + dh_) % 2, (r + dl_) % 2, x, y, c)
        remote(zbuf.at[zc], zbuf.at[zc], 2, dev).start()
    grad_in(1)
    grad_out(1)

    wait_parts(zbuf, 3, ar_r.at[2])
    total = (zbuf[0] + zbuf[1]) + (zbuf[2] + zbuf[3])
    tall = [total[:, t * 128 : (t + 1) * 128] for t in range(3)] + [jnp.zeros((8, 128), F32)]
    me = c * 16 + x * 4 + y
    whole[me] = jnp.concatenate(tall, axis=0).astype(BF)
    for d in sorted(range(1, 32), key=lambda d: -hops(d % 16)):
        xx, yy, cc = (x + (d // 4) % 4) % 4, (y + d % 4) % 4, (c + d // 16) % 2
        remote(whole.at[me], whole.at[me], 3, device(zh, r, xx, yy, cc)).start()
    for b in range(B):
        tokens_grad(b)
    wait_parts(whole, 31, ar_r.at[3])
    for ch in range(2):
        for xy in range(16):
            piece = whole[ch * 16 + xy].astype(F32)
            for t in range(3):
                lane = (xy % 4) * PIECE + t * 128
                if lane < D:
                    gp_out[ch * 4 + xy // 4, :, lane : lane + 128] = piece[t * 8 : t * 8 + 8]

    for half in range(2):
        wait_half(half, msg, ssem)
        wait_half(half, msg2, ssem2)
    to_core.wait_send()
    wait_parts(rs, 15, ar_s.at[1])
    wait_parts(zbuf, 3, ar_s.at[2])
    wait_parts(whole, 31, ar_s.at[3])


def store_kernel(*refs):
    sources, targets, sems = refs[:4], refs[4:8], refs[8]
    copies = []
    for src, dst in zip(sources, targets):
        if len(src.shape) == 3:
            step = 1 if src.shape[0] == B else src.shape[0]
            parts = [pl.ds(n, step) for n in range(0, src.shape[0], step)]
        else:
            parts = [pl.ds(n, 160) for n in range(0, src.shape[0], 160)]
        for part in parts:
            copies.append(pltpu.make_async_copy(src.at[part], dst.at[part], sems.at[len(copies)]))
    for copy in copies:
        copy.start()
    for copy in copies:
        copy.wait()


def body(tokens, slot_params, expert_in, expert_out, grad_out):
    vm = pltpu.VMEM
    dma = pltpu.SemaphoreType.DMA
    scratch = [
        vm((B, M, D), BF), vm((S, D), BF), vm((D, F), BF), vm((F, D), BF), vm((B, M, D), BF),
        vm((R, D), BF), vm((R, M), F32), vm((R, M), F32),
        vm((R, B * M), BF), vm((R, B * M), BF), vm((R, B * M), BF),
        vm((S, 16, HALF), BF), vm((S, 16, HALF), BF),
        vm((S, 16, HALF), BF), vm((S, 16, HALF), BF),
        vm((2, 2, 2, HR, D), BF), vm((2, R, F), BF), vm((2, R, F), BF),
        vm((HALF, R), BF), vm((F // 2, R), BF), vm((2, R, D), BF),
        vm((2, 4, 4, 8, PIECE), F32), vm((4, 4, 8, PIECE), F32), vm((4, 4, 8, PIECE), F32),
        vm((16, 8, PIECE), F32), vm((4, 8, PIECE), F32), vm((32, 32, 128), BF),
        dma((5,)), dma((2,)), dma((2,)), dma((2,)), dma((2,)), dma((2,)), dma((2,)), dma((2,)),
        dma((4,)), dma((4,)), pltpu.SemaphoreType.REGULAR,
    ]
    anywhere = pl.BlockSpec(memory_space=pl.ANY)
    in_vmem = pl.BlockSpec(memory_space=vm)
    shapes = (((B, M, D), BF), ((8, 8, D), F32), ((HALF, F), BF), ((F // 2, D), BF))
    results = pl.pallas_call(
        kernel,
        out_shape=tuple(vm(*shape) for shape in shapes),
        in_specs=[anywhere] * 5,
        out_specs=(in_vmem,) * 4,
        scratch_shapes=scratch,
        compiler_params=pltpu.CompilerParams(
            collective_id=0, has_side_effects=True, vmem_limit_bytes=48 << 20
        ),
    )(tokens, slot_params.T, expert_in[0], expert_out[0], grad_out)
    gt, gp, gi, gw = pl.pallas_call(
        store_kernel,
        out_shape=tuple(jax.ShapeDtypeStruct(*shape) for shape in shapes),
        in_specs=[in_vmem] * 4,
        out_specs=(anywhere,) * 4,
        scratch_shapes=[dma((17,))],
        compiler_params=pltpu.CompilerParams(vmem_limit_bytes=1 << 20),
    )(*(pltpu.with_memory_space_constraint(v, vm) for v in results))
    return gt, gp.reshape(S, D).T, gi[None], gw[None]


def solution(mesh):
    in_specs = (
        P(("rep", "exp"), None, None),
        P(),
        P("exp", None, None),
        P("exp", None, None),
        P(("rep", "exp"), None, None),
    )
    out_specs = (P(("rep", "exp"), None, None), P(), P("exp", "rep", None), P("exp", "rep", None))
    return jax.shard_map(body, mesh=mesh, in_specs=in_specs, out_specs=out_specs, check_vma=False)
```

```python
import math

import jax
import jax.numpy as jnp
from jax import lax
from jax.experimental import pallas as pl
from jax.experimental.pallas import tpu as pltpu
from jax.sharding import PartitionSpec as P

GELU_C = math.sqrt(2.0 / math.pi)
CUBIC = 0.044715
MESH = pl.DeviceIdType.MESH

D = 1280
F = 2560
M = 256
S = 64
HS = S // 2
B = 4
R = S * B
HR = R // 2
HALF = D // 2
BF = jnp.bfloat16
F32 = jnp.float32

def hops(i):
    return (i // 16) % 2 + (0, 1, 2, 1)[(i // 4) % 4] + (0, 1, 2, 1)[i % 4]


FAR_FIRST = sorted(range(HS), key=lambda i: -hops(i))
PIECE = 384

NT = (((1,), (1,)), ((), ()))


def dot(a, b):
    return jnp.dot(a, b, preferred_element_type=F32)


def dot_nt(a, b):
    return lax.dot_general(a, b, NT, preferred_element_type=F32)


def by_parity(buf, half):
    return buf.at[pl.ds(half * HS, HS)].reshape(HS // 2, 2, 16, HALF)


def pack(first, second):
    rows, width = first.shape
    a = first.reshape(rows // 8, 8, width)
    g = second.reshape(rows // 8, 8, width)
    low = lax.broadcasted_iota(jnp.int32, a.shape, 1) < 4
    even = jnp.where(low, a, pltpu.roll(g, 4, 1))
    odd = jnp.where(low, pltpu.roll(a, 4, 1), g)
    return even, odd


def unpack(even, odd):
    rows = even.shape[0] * 8
    low = lax.broadcasted_iota(jnp.int32, even.shape, 1) < 4
    a = jnp.where(low, even, pltpu.roll(odd, 4, 1))
    g = jnp.where(low, pltpu.roll(even, 4, 1), odd)
    return a.reshape(rows, -1), g.reshape(rows, -1)


def columns(p):
    return slice(p * 128, (p + 1) * 128), slice(HALF + p * 128, HALF + (p + 1) * 128)


def store_message(msg, half, p, first, second):
    even, odd = pack(first, second)
    msg = by_parity(msg, half)
    for j, v in enumerate((even, odd)):
        rows = jnp.concatenate([v[:, :, :128], v[:, :, 128:]], axis=1)
        msg[:, j, :, columns(p)[0]] = rows.astype(BF)


def load_message(rcv, half, p):
    rcv = by_parity(rcv, half)
    sides = []
    for j in range(2):
        rows = rcv[:, j, :, columns(p)[0]].astype(F32)
        sides.append(jnp.concatenate([rows[:, :8], rows[:, 8:]], axis=2))
    return unpack(sides[0], sides[1])


def gelu_both(v):
    u = v * v
    t = jnp.tanh(GELU_C * (v + CUBIC * v * u))
    half = 0.5 * (1.0 + t)
    slope = half + 0.5 * v * (1.0 - t * t) * (GELU_C * (1.0 + 3.0 * CUBIC * u))
    return half * v, slope


def kernel(
    tok_hbm, sp_hbm, win_hbm, wout_hbm, gro_hbm,
    gt_out, gp_out, gi_out, gw_out,
    tok, sp, win, wout, gro, wrep, disp, comb, dmask, cmask, dlm,
    msg, rcv, msg2, rcv2, xg, act, dh, xht, actt, ys, gp, cbuf, mine, rs, zbuf, whole,
    in_sems, ssem, rsem, ssem2, rsem2, lsems, fsem, frsem, ar_s, ar_r, sem2,
):
    r = lax.axis_index("rep")
    e = lax.axis_index("exp")
    zh = e // 32
    x = (e // 8) % 4
    y = (e // 2) % 4
    c = e % 2

    def device(zhi, zlo, xx, yy, cc):
        return (zlo, zhi * 32 + xx * 8 + yy * 2 + cc)

    def target(i, sign):
        zb = (i // 16) % 2
        return device(
            (zh + zb) % 2,
            (r + zb) % 2,
            (x + sign * ((i // 4) % 4) + 4) % 4,
            (y + sign * (i % 4) + 4) % 4,
            (c + i // 32) % 2,
        )

    loads = [
        pltpu.make_async_copy(src, dst, in_sems.at[n])
        for n, (src, dst) in enumerate(
            ((tok_hbm, tok), (sp_hbm, sp), (gro_hbm, gro), (win_hbm, win), (wout_hbm, wout))
        )
    ]
    for copy in loads[:3]:
        copy.start()

    row_group = [ic * 32 + ix * 4 for ic in range(2) for ix in range(4) if ic + ix > 0]
    col_group = [zb * 16 + iy for zb in range(2) for iy in range(4) if zb + iy > 0]
    barrier = pltpu.get_barrier_semaphore()
    for i in row_group + col_group:
        pl.semaphore_signal(barrier, inc=1, device_id=target(i, 1), device_id_type=MESH)
    for dev in (device(zh, 1 - r, x, y, c), device(1 - zh, r, x, y, c)):
        pl.semaphore_signal(barrier, inc=1, device_id=dev, device_id_type=MESH)

    def slot_of(i):
        zb = (i // 16) % 2
        return (
            ((zh + zb) % 2) * 32
            + ((x + (i // 4) % 4) % 4) * 8
            + ((y + i % 4) % 4) * 2
            + (c + i // 32) % 2
        )

    row_i = lax.broadcasted_iota(jnp.int32, (R, S), 0) // B
    pick = (slot_of(row_i) == lax.broadcasted_iota(jnp.int32, (R, S), 1)).astype(F32).astype(BF)
    col_i = lax.broadcasted_iota(jnp.int32, (S, R), 1) // B
    pick_t = (slot_of(col_i) == lax.broadcasted_iota(jnp.int32, (S, R), 0)).astype(F32).astype(BF)
    image = lax.broadcasted_iota(jnp.int32, (R, M), 0) % B

    loads[1].wait()
    wrep[...] = dot(pick, sp[...]).astype(BF)
    loads[0].wait()
    logits = jnp.zeros((R, M), F32)
    for b in range(B):
        logits = jnp.where(image == b, dot_nt(wrep[...], tok[b]), logits)

    top = jnp.max(logits, axis=1, keepdims=True)
    p = jnp.exp(logits - top)
    dispatch = p / jnp.sum(p, axis=1, keepdims=True)
    disp[...] = dispatch
    l3 = logits.reshape(R // 8, 8, M)
    top = jnp.max(l3, axis=0)
    top = jnp.maximum(top, pltpu.roll(top, 4, 0))
    p = jnp.exp(l3 - top[None])
    total = jnp.sum(p, axis=0)
    total = total + pltpu.roll(total, 4, 0)
    combine = (p / total[None]).reshape(R, M)
    comb[...] = combine
    for b in range(B):
        dmask[:, b * M : (b + 1) * M] = jnp.where(image == b, dispatch, 0.0).astype(BF)
        cmask[:, b * M : (b + 1) * M] = jnp.where(image == b, combine, 0.0).astype(BF)
    loads[2].wait()
    for copy in loads[3:]:
        copy.start()

    pl.semaphore_wait(barrier, 16)
    for i in row_group:
        pl.semaphore_signal(sem2, inc=1, device_id=target(i, 1), device_id_type=MESH)

    def gather(half):
        rows = slice(half * HR, (half + 1) * HR)
        for p in range(5):
            lo, hi = columns(p)
            rhs = jnp.concatenate([tok[:, :, lo], tok[:, :, hi]], axis=2).reshape(B * M, 256)
            first = dot(dmask[rows, :], rhs)
            rhs = jnp.concatenate([gro[:, :, lo], gro[:, :, hi]], axis=2).reshape(B * M, 256)
            second = dot(cmask[rows, :], rhs)
            store_message(msg, half, p, first, second)

    def send_half(half, src, dst, ssem, rsem, sign):
        for k in FAR_FIRST:
            i = half * HS + k
            if i > 0:
                pltpu.make_async_remote_copy(
                    src_ref=src.at[i],
                    dst_ref=dst.at[i],
                    send_sem=ssem.at[half],
                    recv_sem=rsem.at[half],
                    device_id=target(i, sign),
                    device_id_type=MESH,
                ).start()

    def wait_half(half, buf, sem):
        part = buf.at[pl.ds(half * HS + 1 - half, HS - 1 + half)]
        pltpu.make_async_copy(part, part, sem.at[half]).wait()

    gather(0)
    pl.semaphore_wait(sem2, 7)
    send_half(0, msg, rcv, ssem, rsem, 1)
    own = pltpu.make_async_copy(msg.at[0], rcv.at[0], lsems.at[0])
    own.start()
    gather(1)
    send_half(1, msg, rcv, ssem, rsem, 1)
    loads[3].wait()
    loads[4].wait()
    own.wait()

    def hidden(side, halves):
        rows = slice(halves[0] * HR, (halves[-1] + 1) * HR)
        count = len(halves) * HR
        at_h = slice(halves[0], halves[-1] + 1)
        previous = None
        for j in range(F // 256 + 1):
            current = None
            if j < F // 256:
                at = slice(j * 256, (j + 1) * 256)
                pre = dot(xg[side, at_h, 0].reshape(count, D), win[:, at])
                d_act = dot_nt(xg[side, at_h, 1].reshape(count, D), wout[at, :])
                current = (pre, d_act, at)
            if previous is not None:
                pre, d_act, at = previous
                value, slope = gelu_both(pre)
                act[side, rows, at] = value.astype(BF)
                dh[side, rows, at] = (d_act * slope).astype(BF)
            previous = current

    forwards = []

    def expert(half):
        wait_half(half, rcv, rsem)
        for p in range(5):
            first, second = load_message(rcv, half, p)
            for h, at in enumerate(columns(p)):
                xg[0, half, 0, :, at] = first[:, h * 128 : (h + 1) * 128].astype(BF)
                xg[0, half, 1, :, at] = second[:, h * 128 : (h + 1) * 128].astype(BF)
        forward = pltpu.make_async_remote_copy(
            src_ref=xg.at[0, half],
            dst_ref=xg.at[1, half],
            send_sem=fsem.at[half],
            recv_sem=frsem.at[half],
            device_id=(1 - r, e),
            device_id_type=MESH,
        )
        forward.start()
        forwards.append(forward)
        hidden(0, (half,))
        rows = slice(half * HR, (half + 1) * HR)
        for p in range(5):
            lo, hi = columns(p)
            first = dot(act[0, rows, :], jnp.concatenate([wout[:, lo], wout[:, hi]], axis=1))
            second = dot_nt(dh[0, rows, :], jnp.concatenate([win[lo, :], win[hi, :]], axis=0))
            store_message(msg2, half, p, first, second)
        send_half(half, msg2, rcv2, ssem2, rsem2, -1)

    expert(0)
    own = pltpu.make_async_copy(msg2.at[0], rcv2.at[0], lsems.at[1])
    own.start()
    expert(1)

    my_cols = pl.ds(pl.multiple_of(r * HALF, 128), HALF)
    my_hidden = pl.ds(pl.multiple_of(r * (F // 2), 256), F // 2)

    def grad_in(side):
        xht[...] = xg[side, :, 0, :, my_cols].reshape(R, HALF).T
        for j in range(F // 256):
            at = slice(j * 256, (j + 1) * 256)
            term = dot(xht[...], dh[side, :, at])
            if side == 1:
                term = term + gi_out[:, at].astype(F32)
            gi_out[:, at] = term.astype(BF)

    def grad_out(side):
        actt[...] = act[side, :, my_hidden].T
        for j in range(D // 256):
            at = slice(j * 256, (j + 1) * 256)
            term = dot(actt[...], xg[side, :, 1, :, at].reshape(R, 256))
            if side == 1:
                term = term + gw_out[:, at].astype(F32)
            gw_out[:, at] = term.astype(BF)

    grad_in(0)
    grad_out(0)
    own.wait()
    d_comb, d_disp = [], []
    for half in range(2):
        wait_half(half, rcv2, rsem2)
        rows = slice(half * HR, (half + 1) * HR)
        for p in range(5):
            first, second = load_message(rcv2, half, p)
            for h, at in enumerate(columns(p)):
                ys[0, rows, at] = first[:, h * 128 : (h + 1) * 128].astype(BF)
                ys[1, rows, at] = second[:, h * 128 : (h + 1) * 128].astype(BF)
        of_comb = jnp.zeros((HR, M), F32)
        of_disp = jnp.zeros((HR, M), F32)
        for b in range(B):
            of_comb = jnp.where(image[:HR] == b, dot_nt(ys[0, rows, :], gro[b]), of_comb)
            of_disp = jnp.where(image[:HR] == b, dot_nt(ys[1, rows, :], tok[b]), of_disp)
        d_comb.append(of_comb)
        d_disp.append(of_disp)
    d_comb = jnp.concatenate(d_comb, axis=0)
    d_disp = jnp.concatenate(d_disp, axis=0)
    combine = comb[...].reshape(R // 8, 8, M)
    d_comb = d_comb.reshape(R // 8, 8, M)
    total = jnp.sum(combine * d_comb, axis=0)
    total = total + pltpu.roll(total, 4, 0)
    d_logits = (combine * (d_comb - total[None])).reshape(R, M)
    dispatch = disp[...]
    d_logits = d_logits + dispatch * (
        d_disp - jnp.sum(dispatch * d_disp, axis=1, keepdims=True)
    )
    for b in range(B):
        dlm[:, b * M : (b + 1) * M] = jnp.where(image == b, d_logits, 0.0).astype(BF)
    per_slot = dot(pick_t, dlm[...]).astype(BF)

    zc = zh * 2 + r
    sibling = device(zh, r, x, y, 1 - c)

    def plane(d):
        xx, yy = (x + d // 4) % 4, (y + d % 4) % 4
        return xx, yy, device(zh, r, xx, yy, c)

    plane_far = sorted(range(1, 16), key=lambda d: -hops(d))

    def remote(src, dst, phase, dev):
        return pltpu.make_async_remote_copy(
            src_ref=src,
            dst_ref=dst,
            send_sem=ar_s.at[phase],
            recv_sem=ar_r.at[phase],
            device_id=dev,
            device_id_type=MESH,
        )

    def wait_parts(buf, count, sem):
        part = buf.at[pl.ds(0, count)]
        pltpu.make_async_copy(part, part, sem).wait()

    def tokens_grad(b):
        at = slice(b * M, (b + 1) * M)
        left = jnp.concatenate([dmask[:, at], dlm[:, at]], axis=0).T
        for j in range(D // 256):
            cols = slice(j * 256, (j + 1) * 256)
            right = jnp.concatenate([ys[1, :, cols], wrep[:, cols]], axis=0)
            gt_out[b, :, cols] = dot(left, right).astype(BF)

    for q in range(4):
        width = min(PIECE, D - q * PIECE)
        rhs = tok[:, :, q * PIECE : q * PIECE + width].reshape(B * M, width)
        gp[:, :, q, :, :width] = dot(per_slot, rhs).reshape(2, 4, 8, width)
        if width < PIECE:
            gp[:, :, q, :, width:] = jnp.zeros((2, 4, 8, PIECE - width), F32)
        remote(gp.at[1 - c, :, q], cbuf.at[:, q], 0, sibling).start()
    wait_parts(cbuf, 4, ar_r.at[0])
    mine[...] = gp[c] + cbuf[...]
    for d in plane_far:
        xx, yy, dev = plane(d)
        remote(mine.at[xx, yy], rs.at[x * 4 + y], 1, dev).start()
    rs[x * 4 + y] = mine[x, y]
    for forward in forwards:
        forward.wait()
    hidden(1, (0, 1))

    wait_parts(rs, 15, ar_r.at[1])
    zbuf[zc] = jnp.sum(rs[...], axis=0)
    for dh_, dl_ in ((0, 1), (1, 0), (1, 1)):
        dev = device((zh + dh_) % 2, (r + dl_) % 2, x, y, c)
        remote(zbuf.at[zc], zbuf.at[zc], 2, dev).start()
    grad_in(1)
    grad_out(1)

    wait_parts(zbuf, 3, ar_r.at[2])
    total = (zbuf[0] + zbuf[1]) + (zbuf[2] + zbuf[3])
    tall = [total[:, t * 128 : (t + 1) * 128] for t in range(3)] + [jnp.zeros((8, 128), F32)]
    me = c * 16 + x * 4 + y
    whole[me] = jnp.concatenate(tall, axis=0).astype(BF)
    for d in sorted(range(1, 32), key=lambda d: -hops(d % 16)):
        xx, yy, cc = (x + (d // 4) % 4) % 4, (y + d % 4) % 4, (c + d // 16) % 2
        remote(whole.at[me], whole.at[me], 3, device(zh, r, xx, yy, cc)).start()
    for b in range(B):
        tokens_grad(b)
    wait_parts(whole, 31, ar_r.at[3])
    for ch in range(2):
        for xy in range(16):
            piece = whole[ch * 16 + xy].astype(F32)
            for t in range(3):
                lane = (xy % 4) * PIECE + t * 128
                if lane < D:
                    gp_out[ch * 4 + xy // 4, :, lane : lane + 128] = piece[t * 8 : t * 8 + 8]

    for half in range(2):
        wait_half(half, msg, ssem)
        wait_half(half, msg2, ssem2)
    wait_parts(cbuf, 4, ar_s.at[0])
    wait_parts(rs, 15, ar_s.at[1])
    wait_parts(zbuf, 3, ar_s.at[2])
    wait_parts(whole, 31, ar_s.at[3])


def store_kernel(*refs):
    sources, targets, sems = refs[:4], refs[4:8], refs[8]
    copies = []
    for src, dst in zip(sources, targets):
        if len(src.shape) == 3:
            step = 1 if src.shape[0] == B else src.shape[0]
            parts = [pl.ds(n, step) for n in range(0, src.shape[0], step)]
        else:
            parts = [pl.ds(n, 160) for n in range(0, src.shape[0], 160)]
        for part in parts:
            copies.append(pltpu.make_async_copy(src.at[part], dst.at[part], sems.at[len(copies)]))
    for copy in copies:
        copy.start()
    for copy in copies:
        copy.wait()


def body(tokens, slot_params, expert_in, expert_out, grad_out):
    vm = pltpu.VMEM
    dma = pltpu.SemaphoreType.DMA
    scratch = [
        vm((B, M, D), BF), vm((S, D), BF), vm((D, F), BF), vm((F, D), BF), vm((B, M, D), BF),
        vm((R, D), BF), vm((R, M), F32), vm((R, M), F32),
        vm((R, B * M), BF), vm((R, B * M), BF), vm((R, B * M), BF),
        vm((S, 16, HALF), BF), vm((S, 16, HALF), BF),
        vm((S, 16, HALF), BF), vm((S, 16, HALF), BF),
        vm((2, 2, 2, HR, D), BF), vm((2, R, F), BF), vm((2, R, F), BF),
        vm((HALF, R), BF), vm((F // 2, R), BF), vm((2, R, D), BF),
        vm((2, 4, 4, 8, PIECE), F32), vm((4, 4, 8, PIECE), F32), vm((4, 4, 8, PIECE), F32),
        vm((16, 8, PIECE), F32), vm((4, 8, PIECE), F32), vm((32, 32, 128), BF),
        dma((5,)), dma((2,)), dma((2,)), dma((2,)), dma((2,)), dma((2,)), dma((2,)), dma((2,)),
        dma((4,)), dma((4,)), pltpu.SemaphoreType.REGULAR,
    ]
    anywhere = pl.BlockSpec(memory_space=pl.ANY)
    in_vmem = pl.BlockSpec(memory_space=vm)
    shapes = (((B, M, D), BF), ((8, 8, D), F32), ((HALF, F), BF), ((F // 2, D), BF))
    results = pl.pallas_call(
        kernel,
        out_shape=tuple(vm(*shape) for shape in shapes),
        in_specs=[anywhere] * 5,
        out_specs=(in_vmem,) * 4,
        scratch_shapes=scratch,
        compiler_params=pltpu.CompilerParams(
            collective_id=0, has_side_effects=True, vmem_limit_bytes=48 << 20
        ),
    )(tokens, slot_params.T, expert_in[0], expert_out[0], grad_out)
    gt, gp, gi, gw = pl.pallas_call(
        store_kernel,
        out_shape=tuple(jax.ShapeDtypeStruct(*shape) for shape in shapes),
        in_specs=[in_vmem] * 4,
        out_specs=(anywhere,) * 4,
        scratch_shapes=[dma((17,))],
        compiler_params=pltpu.CompilerParams(vmem_limit_bytes=1 << 20),
    )(*(pltpu.with_memory_space_constraint(v, vm) for v in results))
    return gt, gp.reshape(S, D).T, gi[None], gw[None]


def solution(mesh):
    in_specs = (
        P(("rep", "exp"), None, None),
        P(),
        P("exp", None, None),
        P("exp", None, None),
        P(("rep", "exp"), None, None),
    )
    out_specs = (P(("rep", "exp"), None, None), P(), P("exp", "rep", None), P("exp", "rep", None))
    return jax.shard_map(body, mesh=mesh, in_specs=in_specs, out_specs=out_specs, check_vma=False)
```
